32 devices in a mesh: groups: 2 (over y), band: 4 (over z), dp: 4 (over x, core).
Axes of the slice: x: 2, y: 2, z: 4, core: 2. Of those that a mesh axis runs over, the one named last changes fastest.
Arguments:
- grid_latent: bfloat16 [8, 6144, 512], P(('groups', 'dp'), 'band'), parts along dimension 0, may hold values from -6 to 6
- mesh_latent: bfloat16 [8, 512, 512], P(('groups', 'dp'), 'band'), parts along dimension 0, may hold values from -6 to 6
- cotangent: bfloat16 [8, 512, 512], P(('groups', 'dp'), 'band'), parts along dimension 0, may hold values from -6 to 6
- w_msg: bfloat16 [512, 512], replicated, may hold values from -0.25 to 0.25
- w_self: bfloat16 [512, 512], replicated, may hold values from -0.25 to 0.25
- w_agg: bfloat16 [512, 512], replicated, may hold values from -0.0625 to 0.0625
- w_out: bfloat16 [512, 512], replicated, may hold values from -0.25 to 0.25
- target: int32 [96, 1], P(('groups', 'band')), parts along dimension 0, may hold values from 0 to 3; in each aligned block of 12 rows (0 to 11, 12 to 23, ...) at most 3 rows name the same one
- owner_map: int32 [8], P('groups'), parts along dimension 0, may hold values from 0 to 3, each once
- pattern: int32 [12288, 2], P(('groups', 'band')), parts along dimension 0, may hold values from 0 to 127
- live_blocks: int32 [8], P(('groups', 'band')), parts along dimension 0, may hold values from 6 to 12, as said below
Outputs:
- mesh_out: bfloat16 [8, 512, 512], P(('groups', 'dp'), 'band'), parts along dimension 0
- grad_mesh: bfloat16 [8, 512, 512], P(('groups', 'dp'), 'band'), parts along dimension 0
- grad_grid: bfloat16 [8, 6144, 512], P(('groups', 'dp'), 'band'), parts along dimension 0
- weight_grads: float32 [4096, 512], P(('groups', 'band', 'dp')), parts along dimension 0
The draws below stay inside these ranges and needn't reach their ends.
There are 2 independent parts, one for each index of `groups`. The reference program is written for one: setup_inputs(seed, part) draws one part's arguments, and reference() takes and returns one part's arrays. A program takes and returns all parts, laid end to end along the dimension named above; an argument that names none is the same for every part. Nothing has to cross between parts.
Inputs may be any that keep to these rules, and one draw needn't show every extreme that they name: `target`: in each aligned block of 12 rows (the grid blocks of one band) no mesh block is named more than 3 times, and some mesh block exactly 3 times. `owner_map`: each mesh block has its own position. `live_blocks`: some band has exactly 12 live blocks.
All inputs are finite; a program needn't handle non-finite values.
Results may differ from the reference program's by a relative error of at most 0.0068.
Values may be sent and summed in bfloat16 or wider, within the bound.
A program may use at most 128 MiB of HBM per device.

```python
import math
import jax
import jax.numpy as jnp
import numpy as np
from jax import lax

L = 512
BS = 128
GB_DEV = 12
MBLOCKS = 4
GBLOCKS = 48
GRID = 6144
MESH = 512
CAP = 3
SAMPLES = 4
N_BAND = 4


def draw_live_blocks(key, part):
    key = jax.random.fold_in(key, 7)
    lowest = max(1, GB_DEV // 2)
    counts = jax.random.randint(jax.random.fold_in(key, 1), (N_BAND,), lowest, GB_DEV + 1, dtype=jnp.int32)
    fullest = jax.random.randint(jax.random.fold_in(key, 2), (), 0, N_BAND, dtype=jnp.int32)
    band_ids = jnp.arange(N_BAND, dtype=jnp.int32)
    return jnp.where(band_ids == fullest, GB_DEV, counts).astype(jnp.int32)


def place_ends(array, stream_key, low, largest):
    place = [jax.random.randint(jax.random.fold_in(stream_key, axis), (), 0, length) for axis, length in enumerate(array.shape)]
    widest = array.shape.index(max(array.shape))
    next_to = place[:widest] + [(place[widest] + 1) % array.shape[widest]] + place[widest + 1:]
    return array.at[tuple(place)].set(low).at[tuple(next_to)].set(largest)


def levels(own_key, extent, shards, low, largest):
    def one(position, shards_of):
        draws = jax.random.uniform(jax.random.fold_in(jax.random.fold_in(own_key, 6), position), (shards_of,), jnp.float32, low / len(shards), largest / len(shards))
        return jnp.repeat(jnp.exp(draws), extent[position] // shards_of).reshape((-1,) + (1,) * (len(extent) - position - 1))

    factor_of = one(*shards[0])
    for cut in shards[1:]:
        factor_of = factor_of * one(*cut)
    return factor_of


def routed_block(key, own, number, rows, amount, top, limit, skew):
    ranking = jax.random.permutation(key, amount)
    crowded, usual = load_shares(amount, rows * top, limit, skew, True), load_shares(amount, rows * top, limit, skew, False)
    places = jnp.arange(amount)

    def named(lengths, offset_by):
        used = int((lengths > 0).sum())
        fixed = max(1, used // 4)
        shifted = fixed + (places - fixed + offset_by * (used - fixed)) % max(1, amount - fixed)
        return jnp.zeros((amount,), jnp.int32).at[ranking[jnp.where(places < fixed, places, shifted)]].set(jnp.asarray(lengths, jnp.int32))

    lengths = jnp.where(number % 4 == 0, named(crowded, number // 4), named(usual, number - number // 4 - 1))
    mixed = jax.random.permutation(jax.random.fold_in(own, 3), amount)
    donor, sink = mixed[0:amount // 2 * 2:2], mixed[1:amount // 2 * 2:2]
    margin = jnp.minimum(lengths[donor] - 1, limit - lengths[sink]) // 2
    margin = jnp.where((donor == ranking[0]) | (sink == ranking[0]) | (lengths[sink] == 0), 0, jnp.maximum(margin, 0))
    shifted = jax.random.randint(jax.random.fold_in(own, 4), (amount // 2,), 0, 1 << 20) % (margin + 1)
    lengths = lengths.at[donor].add(-shifted).at[sink].add(shifted)
    items = jnp.searchsorted(jnp.cumsum(lengths), jnp.arange(rows * top), side="right").astype(jnp.int32)
    grid = items.reshape(top, rows).T
    grid = grid[jax.random.permutation(jax.random.fold_in(own, 1), rows)]
    offset_by = jax.random.randint(jax.random.fold_in(own, 2), (rows, 1), 0, top)
    return jnp.take_along_axis(grid, (jnp.arange(top)[None, :] + offset_by) % top, axis=1)


def load_shares(number_of, total, bound, lean, full):
    portions = [(1 << 20) // math.isqrt(rank ** lean) + 1 for rank in range(1, number_of + 1)]
    largest = bound if full else min(bound, max(-(-total // number_of), total * portions[0] // sum(portions)))
    least = 1 if total - largest >= number_of - 1 else 0
    given, surplus = [largest] + [least] * (number_of - 1), total - largest - least * (number_of - 1)
    while surplus > 0:
        free = [i for i in range(1, number_of) if given[i] < largest] or [i for i in range(1, number_of) if given[i] < bound]
        mass, left = sum([portions[i] for i in free]), surplus
        for i in free:
            addition = min(bound - given[i], max(1, left * portions[i] // mass), surplus)
            given[i] = given[i] + addition
            surplus = surplus - addition
    return np.array(given)


def scatter_about(stream_key, shape, spread, reach, pieces=(), kind=jnp.bfloat16):
    gain = levels(stream_key, shape, pieces, -0.22, 0.18) if pieces else 1.0
    array = jax.random.normal(stream_key, shape, jnp.float32) * spread * gain
    return jnp.minimum(jnp.maximum(array, -reach), reach).astype(kind)


def setup_inputs(seed: int = 0, part: int = 0) -> dict:
    streams_of = jax.random.split(jax.random.key(seed), 12)
    part_keys = jax.random.split(jax.random.fold_in(streams_of[11], part), 12)
    grid_latent = scatter_about(part_keys[0], (SAMPLES, GRID, L), 1.0, 6.0, ((0, 4), (1, 4)))
    mesh_latent = scatter_about(part_keys[1], (SAMPLES, MESH, L), 1.0, 6.0, ((0, 4), (1, 4)))
    cotangent = scatter_about(part_keys[2], (SAMPLES, MESH, L), 1.0, 6.0, ((0, 4), (1, 4)))
    w_msg = scatter_about(streams_of[3], (L, L), L ** -0.5, 0.25)
    w_self = scatter_about(streams_of[4], (L, L), L ** -0.5, 0.25)
    w_agg = scatter_about(streams_of[5], (L, L), (16 * L) ** -0.5, 0.0625)
    w_out = scatter_about(streams_of[6], (L, L), L ** -0.5, 0.25)
    target_keys = jax.random.split(jax.random.fold_in(part_keys[7], 1), GBLOCKS // GB_DEV)
    target_turns = jax.random.permutation(jax.random.fold_in(part_keys[7], 3), GBLOCKS // GB_DEV)
    target = jax.vmap(lambda own, number: routed_block(jax.random.fold_in(part_keys[7], 2), own, number, GB_DEV, MBLOCKS, 1, CAP, 2))(target_keys, target_turns).reshape((GBLOCKS, 1))
    owner_map = jax.random.permutation(part_keys[8], MBLOCKS).astype(jnp.int32)
    pattern = place_ends(jax.random.randint(part_keys[9], (GRID, 2), 0, BS), jax.random.fold_in(part_keys[9], 1), 0, BS - 1).astype(jnp.int32)
    live_blocks = draw_live_blocks(jax.random.fold_in(jax.random.fold_in(streams_of[11], part), 71), part)
    return {"grid_latent": grid_latent, "mesh_latent": mesh_latent, "cotangent": cotangent, "w_msg": w_msg, "w_self": w_self, "w_agg": w_agg, "w_out": w_out, "target": target, "owner_map": owner_map, "pattern": pattern, "live_blocks": live_blocks}


def silu_slope(value):
    logistic = jax.nn.sigmoid(value)
    return logistic * (1.0 + value * (1.0 - logistic))


def reference(grid_latent, mesh_latent, cotangent, w_msg, w_self, w_agg, w_out, target, owner_map, pattern, live_blocks):
    block_ids = jnp.arange(GBLOCKS, dtype=jnp.int32)
    live_flag = (block_ids % GB_DEV) < live_blocks[block_ids // GB_DEV]
    mesh_slot = owner_map[target[:, 0]]
    node_slot = jnp.repeat(mesh_slot, BS)
    node_live = jnp.repeat(live_flag, BS).astype(jnp.float32)[:, None]
    rows_first = node_slot * BS + pattern[:, 0]
    rows_second = node_slot * BS + pattern[:, 1]

    def one_sample(inputs):
        grid_rows, mesh_rows, cot_rows = inputs
        pre_msg = jnp.dot(grid_rows, w_msg, preferred_element_type=jnp.float32)
        messages = jax.nn.silu(pre_msg).astype(jnp.bfloat16)
        weighted = messages.astype(jnp.float32) * node_live
        aggregate = jnp.zeros((MESH, L), jnp.float32).at[rows_first].add(weighted).at[rows_second].add(weighted)
        agg_half = aggregate.astype(jnp.bfloat16)
        pre_hidden = jnp.dot(mesh_rows, w_self, preferred_element_type=jnp.float32) + jnp.dot(agg_half, w_agg, preferred_element_type=jnp.float32)
        hidden = jax.nn.silu(pre_hidden).astype(jnp.bfloat16)
        mesh_out = (mesh_rows.astype(jnp.float32) + jnp.dot(hidden, w_out, preferred_element_type=jnp.float32)).astype(jnp.bfloat16)
        d_hidden = jnp.dot(cot_rows, w_out.T, preferred_element_type=jnp.float32)
        d_pre_hidden = (d_hidden * silu_slope(pre_hidden)).astype(jnp.bfloat16)
        grad_mesh = (cot_rows.astype(jnp.float32) + jnp.dot(d_pre_hidden, w_self.T, preferred_element_type=jnp.float32)).astype(jnp.bfloat16)
        d_aggregate = jnp.dot(d_pre_hidden, w_agg.T, preferred_element_type=jnp.float32).astype(jnp.bfloat16)
        d_wide = d_aggregate.astype(jnp.float32)
        d_messages = (d_wide[rows_first] + d_wide[rows_second]) * node_live
        d_pre_msg = (d_messages * silu_slope(pre_msg)).astype(jnp.bfloat16)
        grad_grid = jnp.dot(d_pre_msg, w_msg.T, preferred_element_type=jnp.float32).astype(jnp.bfloat16)
        stacked = jnp.concatenate([
            jnp.dot(mesh_rows.T, d_pre_hidden, preferred_element_type=jnp.float32),
            jnp.dot(agg_half.T, d_pre_hidden, preferred_element_type=jnp.float32),
            jnp.dot(hidden.T, cot_rows, preferred_element_type=jnp.float32),
            jnp.dot(grid_rows.T, d_pre_msg, preferred_element_type=jnp.float32)], axis=0)
        return mesh_out, grad_mesh, grad_grid, stacked

    mesh_out, grad_mesh, grad_grid, stacked = lax.map(one_sample, (grid_latent, mesh_latent, cotangent))
    return mesh_out, grad_mesh, grad_grid, jnp.sum(stacked, axis=0)
```

```python
import functools
import jax
import jax.numpy as jnp
from jax import lax
from jax.experimental import pallas as pl
from jax.experimental.pallas import tpu as pltpu
from jax.sharding import PartitionSpec as P

MESH = pl.DeviceIdType.MESH
F32 = jnp.float32
BF16 = jnp.bfloat16


def silu_slope(value):
    logistic = jax.nn.sigmoid(value)
    return logistic * (1.0 + value * (1.0 - logistic))


def incidence_of(edge_pattern, block_size):
    columns = jnp.arange(block_size, dtype=jnp.int32)
    first_hit = (edge_pattern[..., 0:1] == columns).astype(jnp.bfloat16)
    second_hit = (edge_pattern[..., 1:2] == columns).astype(jnp.bfloat16)
    return first_hit + second_hit


def row_product(left, right):
    return lax.dot_general(
        left, right, (((0,), (0,)), ((), ())), preferred_element_type=jnp.float32
    )


def shards(
    grid_latent,
    mesh_latent,
    cotangent,
    w_msg,
    w_self,
    w_agg,
    w_out,
    target,
    owner_map,
    pattern,
    live_blocks,
):
    grid_rows = grid_latent[0]
    mesh_rows = mesh_latent[0]
    cot_rows = cotangent[0]
    block_count = target.shape[0]
    width = grid_rows.shape[1]
    block_size = grid_rows.shape[0] // block_count
    bands = lax.axis_size("band")
    mesh_blocks = owner_map.shape[0]
    per_band = mesh_blocks // bands
    capacity = (block_count + mesh_blocks - 1) // mesh_blocks
    slot_total = mesh_blocks * capacity
    block_ids = jnp.arange(block_count, dtype=jnp.int32)
    live_flag = block_ids < live_blocks[0]
    matches = target[:, 0][:, None] == jnp.arange(mesh_blocks, dtype=jnp.int32)[None, :]
    mesh_slot = jnp.sum(jnp.where(matches, owner_map[None, :], 0), axis=1)
    same_slot = (
        (mesh_slot[:, None] == mesh_slot[None, :])
        & live_flag[None, :]
        & (block_ids[None, :] < block_ids[:, None])
    )
    slot_rank = jnp.sum(same_slot.astype(jnp.int32), axis=1)
    buffer_index = jnp.where(live_flag, mesh_slot * capacity + slot_rank, slot_total)
    pre_msg = jnp.dot(grid_rows, w_msg, preferred_element_type=jnp.float32)
    messages = jax.nn.silu(pre_msg).astype(jnp.bfloat16).reshape(block_count, block_size, width)
    local_pattern = pattern.reshape(block_count, block_size, 2)
    send_msgs = (
        jnp.zeros((slot_total, block_size, width), jnp.bfloat16)
        .at[buffer_index]
        .set(messages, mode="drop")
    )
    send_pattern = (
        jnp.zeros((slot_total, block_size, 2), jnp.int32)
        .at[buffer_index]
        .set(local_pattern, mode="drop")
    )
    recv_msgs, recv_pattern = (
        lax.all_to_all(send_msgs, "band", split_axis=0, concat_axis=0, tiled=True),
        lax.all_to_all(send_pattern, "band", split_axis=0, concat_axis=0, tiled=True),
    )
    recv_incidence = incidence_of(recv_pattern, block_size).reshape(
        bands, per_band, capacity, block_size, block_size
    )
    aggregate = jnp.einsum(
        "pmcgk,pmcgl->mkl",
        recv_incidence,
        recv_msgs.reshape(bands, per_band, capacity, block_size, width),
        preferred_element_type=jnp.float32,
    )
    agg_half = aggregate.reshape(per_band * block_size, width).astype(jnp.bfloat16)
    pre_hidden = jnp.dot(mesh_rows, w_self, preferred_element_type=jnp.float32) + jnp.dot(
        agg_half, w_agg, preferred_element_type=jnp.float32
    )
    hidden = jax.nn.silu(pre_hidden).astype(jnp.bfloat16)
    mesh_out = (
        mesh_rows.astype(jnp.float32) + jnp.dot(hidden, w_out, preferred_element_type=jnp.float32)
    ).astype(jnp.bfloat16)
    d_hidden = lax.dot_general(
        cot_rows, w_out, (((1,), (1,)), ((), ())), preferred_element_type=jnp.float32
    )
    d_pre_hidden = (d_hidden * silu_slope(pre_hidden)).astype(jnp.bfloat16)
    grad_mesh = (
        cot_rows.astype(jnp.float32)
        + lax.dot_general(
            d_pre_hidden, w_self, (((1,), (1,)), ((), ())), preferred_element_type=jnp.float32
        )
    ).astype(jnp.bfloat16)
    d_aggregate = lax.dot_general(
        d_pre_hidden, w_agg, (((1,), (1,)), ((), ())), preferred_element_type=jnp.float32
    ).astype(jnp.bfloat16)
    d_blocks = d_aggregate.reshape(per_band, block_size, width)
    slot_adjoint = jnp.einsum(
        "pmcgk,mkl->pmcgl", recv_incidence, d_blocks, preferred_element_type=jnp.float32
    )
    returned = lax.all_to_all(
        slot_adjoint.reshape(slot_total, block_size, width),
        "band",
        split_axis=0,
        concat_axis=0,
        tiled=True,
    )
    d_messages = returned[jnp.minimum(buffer_index, slot_total - 1)]
    d_messages = d_messages * live_flag.astype(jnp.float32)[:, None, None]
    d_pre_msg = (d_messages.reshape(block_count * block_size, width) * silu_slope(pre_msg)).astype(
        jnp.bfloat16
    )
    grad_grid = lax.dot_general(
        d_pre_msg, w_msg, (((1,), (1,)), ((), ())), preferred_element_type=jnp.float32
    ).astype(jnp.bfloat16)
    stacked = jnp.concatenate(
        [
            row_product(mesh_rows, d_pre_hidden),
            row_product(agg_half, d_pre_hidden),
            row_product(hidden, cot_rows),
            row_product(grid_rows, d_pre_msg),
        ],
        axis=0,
    )
    weight_grads = lax.psum_scatter(stacked, ("band", "dp"), scatter_dimension=0, tiled=True)
    return (mesh_out[None], grad_mesh[None], grad_grid[None], weight_grads)


def mm(left, right):
    return jnp.dot(left, right, preferred_element_type=F32)


def mm_t(left, right):
    return lax.dot_general(left, right, (((1,), (1,)), ((), ())), preferred_element_type=F32)


def logistic_of(value):
    return 0.5 + 0.5 * jnp.tanh(0.5 * value)


def fused(
    bands,
    tile,
    target_s,
    owner_s,
    live_s,
    pattern_t,
    pattern,
    grid_h,
    mesh_h,
    cot_h,
    wm_h,
    ws_h,
    wa_h,
    wo_h,
    mesh_out_h,
    grad_mesh_h,
    grad_grid_h,
    wg_h,
    grid_v,
    mesh_v,
    cot_v,
    wm_v,
    ws_v,
    wa_v,
    wo_v,
    hits,
    hits_t,
    grid_t,
    msgs,
    slope,
    part,
    part_send,
    part_recv,
    dagg_all,
    dpm,
    gg_v,
    mesh_out_v,
    grad_mesh_v,
    sums,
    send_a,
    recv_a,
    send_b,
    recv_b,
    send_c,
    recv_c,
    total_c,
    wg_v,
    in_sem,
    grid_sem,
    out_sem,
    gg_sem,
    part_ss,
    part_rs,
    dagg_ss,
    dagg_rs,
    a_ss,
    a_rs,
    b_ss,
    b_rs,
    c_ss,
    c_rs,
):
    me = lax.axis_index("band")
    dp = lax.axis_index("dp")
    core = dp % 2
    column = dp // 2
    core_mate = dp + 1 - 2 * core
    x_mate = (dp + 2) % 4
    nodes, width = grid_v.shape
    block = mesh_v.shape[0]
    mesh_rows = hits.shape[0]
    tiles = nodes // tile
    half = width // 2
    blocks = nodes // block

    loads = [
        pltpu.make_async_copy(src, dst, in_sem.at[i])
        for i, (src, dst) in enumerate(
            ((wm_h, wm_v), (mesh_h, mesh_v), (cot_h, cot_v), (ws_h, ws_v), (wa_h, wa_v), (wo_h, wo_v))
        )
    ]

    def grid_load(t):
        rows = pl.ds(t * tile, tile)
        return pltpu.make_async_copy(grid_h.at[rows], grid_v.at[rows], grid_sem.at[t])

    loads[0].start()
    for t in range(tiles):
        grid_load(t).start()
    for load in loads[1:]:
        load.start()

    barrier = pltpu.get_barrier_semaphore()
    for rel in range(1, bands):
        pl.semaphore_signal(
            barrier, inc=1, device_id={"band": (me + rel) % bands}, device_id_type=MESH
        )
    pl.semaphore_signal(barrier, inc=1, device_id={"dp": core_mate}, device_id_type=MESH)
    pl.semaphore_signal(barrier, inc=1, device_id={"dp": x_mate}, device_id_type=MESH)

    live = live_s[0]
    offsets = []
    for k in range(blocks):
        position = owner_s[target_s[k]]
        offsets.append(jnp.where(k < live, position * block, -2 * mesh_rows))
    row_ids = lax.broadcasted_iota(jnp.int32, (mesh_rows, block), 0)
    for k in range(blocks):
        cols = pl.ds(k * block, block)
        first = pattern_t[0:1, cols] + offsets[k]
        second = pattern_t[1:2, cols] + offsets[k]
        hits[:, cols] = (
            (row_ids == first).astype(F32) + (row_ids == second).astype(F32)
        ).astype(BF16)

    loads[0].wait()

    @pl.loop(0, tiles)
    def _(t):
        rows = pl.ds(pl.multiple_of(t * tile, tile), tile)
        grid_load(t).wait()
        pre = mm(grid_v[rows, :], wm_v[...])
        gate = logistic_of(pre)
        msgs[rows, :] = (pre * gate).astype(BF16)
        slope[rows, :] = gate * (1.0 + pre * (1.0 - gate))

    def part_copy(h, rel):
        other = (me + rel) % bands
        return pltpu.make_async_remote_copy(
            src_ref=part_send.at[h, pl.ds(pl.multiple_of(other * block, block), block)],
            dst_ref=part_recv.at[h, rel - 1],
            send_sem=part_ss.at[h, rel - 1],
            recv_sem=part_rs.at[h, rel - 1],
            device_id={"band": other},
            device_id_type=MESH,
        )

    rels = (2, 1, 3)
    for h in range(2):
        cols = slice(h * half, (h + 1) * half)
        partial = mm(hits[...], msgs[:, cols])
        part[:, cols] = partial
        part_send[h] = partial.astype(BF16)
        if h == 0:
            pl.semaphore_wait(barrier, bands + 1)
        for rel in rels:
            part_copy(h, rel).start()

    for load in loads[1:]:
        load.wait()
    mesh_rows_v = mesh_v[...]
    cot_rows = cot_v[...]
    pre_self = mm(mesh_rows_v, ws_v[...])
    d_hidden = mm_t(cot_rows, wo_v[...])

    col_ids = lax.broadcasted_iota(jnp.int32, (block, mesh_rows), 1)
    for k in range(blocks):
        rows = pl.ds(k * block, block)
        first = pattern[rows, 0:1] + offsets[k]
        second = pattern[rows, 1:2] + offsets[k]
        hits_t[rows, :] = (
            (col_ids == first).astype(F32) + (col_ids == second).astype(F32)
        ).astype(BF16)
    for t in range(tiles):
        grid_t[:, t * tile : (t + 1) * tile] = grid_v[t * tile : (t + 1) * tile, :].T

    own = pl.ds(pl.multiple_of(me * block, block), block)
    agg_parts = []
    for h in range(2):
        total = part[own, h * half : (h + 1) * half]
        for rel in rels:
            part_copy(h, rel).wait_recv()
            total = total + part_recv[h, rel - 1].astype(F32)
        agg_parts.append(total.astype(BF16))
    agg = jnp.concatenate(agg_parts, axis=1)
    pre_hidden = pre_self + mm(agg, wa_v[...])
    gate = logistic_of(pre_hidden)
    hidden = (pre_hidden * gate).astype(BF16)
    dph = (d_hidden * (gate * (1.0 + pre_hidden * (1.0 - gate)))).astype(BF16)
    dagg_all[own, :] = mm_t(dph, wa_v[...]).astype(BF16)

    def dagg_copy(rel):
        return pltpu.make_async_remote_copy(
            src_ref=dagg_all.at[own],
            dst_ref=dagg_all.at[own],
            send_sem=dagg_ss.at[rel - 1],
            recv_sem=dagg_rs.at[rel - 1],
            device_id={"band": (me + rel) % bands},
            device_id_type=MESH,
        )

    for rel in rels:
        dagg_copy(rel).start()

    def a_copy(b):
        return pltpu.make_async_remote_copy(
            src_ref=send_a.at[b],
            dst_ref=recv_a.at[b],
            send_sem=a_ss.at[b],
            recv_sem=a_rs.at[b],
            device_id={"dp": core_mate},
            device_id_type=MESH,
        )

    def b_copy(b):
        return pltpu.make_async_remote_copy(
            src_ref=send_b.at[b],
            dst_ref=recv_b.at[b],
            send_sem=b_ss.at[b],
            recv_sem=b_rs.at[b],
            device_id={"dp": x_mate},
            device_id_type=MESH,
        )

    def c_copy(rel):
        other = (me + rel) % bands
        return pltpu.make_async_remote_copy(
            src_ref=send_c.at[other],
            dst_ref=recv_c.at[rel - 1],
            send_sem=c_ss.at[rel - 1],
            recv_sem=c_rs.at[rel - 1],
            device_id={"band": other},
            device_id_type=MESH,
        )

    share = width // 4

    def share_of(b, x, c):
        return sums[b, pl.ds(pl.multiple_of((x * 2 + c) * share, share), share), :]

    def step_a(b):
        for x in range(2):
            send_a[b, x] = share_of(b, x, 1 - core).astype(BF16)
        a_copy(b).start()

    def step_b(b):
        a_copy(b).wait_recv()
        away = 1 - column
        send_b[b] = (share_of(b, away, core) + recv_a[b, away].astype(F32)).astype(BF16)
        b_copy(b).start()

    def step_c(b):
        kept = share_of(b, column, core) + recv_a[b, column].astype(F32)
        b_copy(b).wait_recv()
        kept = kept + recv_b[b].astype(F32)
        total_c[b] = kept
        send_c[b] = kept.astype(BF16)

    sums[0] = row_product(mesh_rows_v, dph)
    step_a(0)
    sums[1] = row_product(agg, dph)
    step_a(1)
    sums[2] = row_product(hidden, cot_rows)
    step_a(2)
    mesh_out_v[...] = (mesh_rows_v.astype(F32) + mm(hidden, wo_v[...])).astype(BF16)
    grad_mesh_v[...] = (cot_rows.astype(F32) + mm_t(dph, ws_v[...])).astype(BF16)
    stores = [
        pltpu.make_async_copy(mesh_out_v, mesh_out_h, out_sem.at[0]),
        pltpu.make_async_copy(grad_mesh_v, grad_mesh_h, out_sem.at[1]),
    ]
    for store in stores:
        store.start()
    for b in range(3):
        step_b(b)
    for b in range(3):
        step_c(b)
    for rel in rels:
        dagg_copy(rel).wait_recv()
    for rel in rels:

        @pl.when((me + rel) % bands != 3)
        def _():
            c_copy(rel).start()

    @pl.loop(0, tiles)
    def _(t):
        rows = pl.ds(pl.multiple_of(t * tile, tile), tile)
        d_msg = mm(hits_t[rows, :], dagg_all[...])
        dpm[rows, :] = (d_msg * slope[rows, :]).astype(BF16)

    for h in range(2):
        cols = slice(h * half, (h + 1) * half)
        sums[3, :, cols] = mm(grid_t[...], dpm[:, cols])
    step_a(3)

    def gg_store(t):
        rows = pl.ds(pl.multiple_of(t * tile, tile), tile)
        return pltpu.make_async_copy(gg_v.at[rows], grad_grid_h.at[rows], gg_sem.at[t])

    def grid_grads(low, high):
        @pl.loop(low, high)
        def _(t):
            rows = pl.ds(pl.multiple_of(t * tile, tile), tile)
            gg_v[rows, :] = mm_t(dpm[rows, :], wm_v[...]).astype(BF16)
            gg_store(t).start()

    grid_grads(0, tiles // 3)
    step_b(3)
    grid_grads(tiles // 3, tiles)
    step_c(3)
    for rel in rels:

        @pl.when((me + rel) % bands == 3)
        def _():
            c_copy(rel).start()

    total = total_c[me]
    for rel in rels:
        c_copy(rel).wait_recv()
        total = total + recv_c[rel - 1].astype(F32)
    wg_v[...] = total
    last = pltpu.make_async_copy(wg_v, wg_h, out_sem.at[2])
    last.start()
    for store in stores:
        store.wait()

    @pl.loop(0, tiles)
    def _(t):
        gg_store(t).wait()

    for rel in rels:
        for h in range(2):
            part_copy(h, rel).wait_send()
        dagg_copy(rel).wait_send()
        c_copy(rel).wait_send()
    for b in range(4):
        a_copy(b).wait_send()
        b_copy(b).wait_send()
    last.wait()


def fused_shards(
    grid_latent,
    mesh_latent,
    cotangent,
    w_msg,
    w_self,
    w_agg,
    w_out,
    target,
    owner_map,
    pattern,
    live_blocks,
):
    bands = lax.axis_size("band")
    nodes, width = grid_latent.shape[1:]
    block = mesh_latent.shape[1]
    rows = bands * block
    tile = 2 * block
    tiles = nodes // tile
    half = width // 2
    share = width // 4
    anywhere = pl.BlockSpec(memory_space=pl.ANY)
    scalars = pl.BlockSpec(memory_space=pltpu.SMEM)
    local = pl.BlockSpec(memory_space=pltpu.VMEM)
    dma = pltpu.SemaphoreType.DMA
    mesh_out, grad_mesh, grad_grid, weight_grads = pl.pallas_call(
        functools.partial(fused, bands, tile),
        out_shape=(
            jax.ShapeDtypeStruct((block, width), BF16),
            jax.ShapeDtypeStruct((block, width), BF16),
            jax.ShapeDtypeStruct((nodes, width), BF16),
            jax.ShapeDtypeStruct((share, width), F32),
        ),
        in_specs=[scalars] * 3 + [local] * 2 + [anywhere] * 7,
        out_specs=(anywhere,) * 4,
        scratch_shapes=[
            pltpu.VMEM((nodes, width), BF16),
            pltpu.VMEM((block, width), BF16),
            pltpu.VMEM((block, width), BF16),
            pltpu.VMEM((width, width), BF16),
            pltpu.VMEM((width, width), BF16),
            pltpu.VMEM((width, width), BF16),
            pltpu.VMEM((width, width), BF16),
            pltpu.VMEM((rows, nodes), BF16),
            pltpu.VMEM((nodes, rows), BF16),
            pltpu.VMEM((width, nodes), BF16),
            pltpu.VMEM((nodes, width), BF16),
            pltpu.VMEM((nodes, width), F32),
            pltpu.VMEM((rows, width), F32),
            pltpu.VMEM((2, rows, half), BF16),
            pltpu.VMEM((2, bands - 1, block, half), BF16),
            pltpu.VMEM((rows, width), BF16),
            pltpu.VMEM((nodes, width), BF16),
            pltpu.VMEM((nodes, width), BF16),
            pltpu.VMEM((block, width), BF16),
            pltpu.VMEM((block, width), BF16),
            pltpu.VMEM((4, width, width), F32),
            pltpu.VMEM((4, 2, share, width), BF16),
            pltpu.VMEM((4, 2, share, width), BF16),
            pltpu.VMEM((4, share, width), BF16),
            pltpu.VMEM((4, share, width), BF16),
            pltpu.VMEM((4, share, width), BF16),
            pltpu.VMEM((bands - 1, share, width), BF16),
            pltpu.VMEM((4, share, width), F32),
            pltpu.VMEM((share, width), F32),
            dma((6,)),
            dma((tiles,)),
            dma((3,)),
            dma((tiles,)),
            dma((2, bands - 1)),
            dma((2, bands - 1)),
            dma((bands - 1,)),
            dma((bands - 1,)),
            dma((4,)),
            dma((4,)),
            dma((4,)),
            dma((4,)),
            dma((bands - 1,)),
            dma((bands - 1,)),
        ],
        compiler_params=pltpu.CompilerParams(
            collective_id=0, has_side_effects=True, vmem_limit_bytes=50 * 2**20
        ),
        name="encoder_step",
    )(
        target[:, 0],
        owner_map,
        live_blocks,
        pattern.T,
        pattern,
        grid_latent[0],
        mesh_latent[0],
        cotangent[0],
        w_msg,
        w_self,
        w_agg,
        w_out,
    )
    return mesh_out[None], grad_mesh[None], grad_grid[None], weight_grads


def solution(mesh):
    in_specs = (
        P(("groups", "dp"), "band", None),
        P(("groups", "dp"), "band", None),
        P(("groups", "dp"), "band", None),
        P(),
        P(),
        P(),
        P(),
        P(("groups", "band"), None),
        P("groups"),
        P(("groups", "band"), None),
        P(("groups", "band")),
    )
    out_specs = (
        P(("groups", "dp"), "band", None),
        P(("groups", "dp"), "band", None),
        P(("groups", "dp"), "band", None),
        P(("groups", "band", "dp"), None),
    )
    body = fused_shards if mesh.shape["band"] == 4 and mesh.shape["dp"] == 4 else shards
    return jax.shard_map(body, mesh=mesh, in_specs=in_specs, out_specs=out_specs, check_vma=False)
```

```python
import functools
import jax
import jax.numpy as jnp
from jax import lax
from jax.experimental import pallas as pl
from jax.experimental.pallas import tpu as pltpu
from jax.sharding import PartitionSpec as P

MESH = pl.DeviceIdType.MESH
F32 = jnp.float32
BF16 = jnp.bfloat16


def silu_slope(value):
    logistic = jax.nn.sigmoid(value)
    return logistic * (1.0 + value * (1.0 - logistic))


def incidence_of(edge_pattern, block_size):
    columns = jnp.arange(block_size, dtype=jnp.int32)
    first_hit = (edge_pattern[..., 0:1] == columns).astype(jnp.bfloat16)
    second_hit = (edge_pattern[..., 1:2] == columns).astype(jnp.bfloat16)
    return first_hit + second_hit


def row_product(left, right):
    return lax.dot_general(
        left, right, (((0,), (0,)), ((), ())), preferred_element_type=jnp.float32
    )


def shards(
    grid_latent,
    mesh_latent,
    cotangent,
    w_msg,
    w_self,
    w_agg,
    w_out,
    target,
    owner_map,
    pattern,
    live_blocks,
):
    grid_rows = grid_latent[0]
    mesh_rows = mesh_latent[0]
    cot_rows = cotangent[0]
    block_count = target.shape[0]
    width = grid_rows.shape[1]
    block_size = grid_rows.shape[0] // block_count
    bands = lax.axis_size("band")
    mesh_blocks = owner_map.shape[0]
    per_band = mesh_blocks // bands
    capacity = (block_count + mesh_blocks - 1) // mesh_blocks
    slot_total = mesh_blocks * capacity
    block_ids = jnp.arange(block_count, dtype=jnp.int32)
    live_flag = block_ids < live_blocks[0]
    matches = target[:, 0][:, None] == jnp.arange(mesh_blocks, dtype=jnp.int32)[None, :]
    mesh_slot = jnp.sum(jnp.where(matches, owner_map[None, :], 0), axis=1)
    same_slot = (
        (mesh_slot[:, None] == mesh_slot[None, :])
        & live_flag[None, :]
        & (block_ids[None, :] < block_ids[:, None])
    )
    slot_rank = jnp.sum(same_slot.astype(jnp.int32), axis=1)
    buffer_index = jnp.where(live_flag, mesh_slot * capacity + slot_rank, slot_total)
    pre_msg = jnp.dot(grid_rows, w_msg, preferred_element_type=jnp.float32)
    messages = jax.nn.silu(pre_msg).astype(jnp.bfloat16).reshape(block_count, block_size, width)
    local_pattern = pattern.reshape(block_count, block_size, 2)
    send_msgs = (
        jnp.zeros((slot_total, block_size, width), jnp.bfloat16)
        .at[buffer_index]
        .set(messages, mode="drop")
    )
    send_pattern = (
        jnp.zeros((slot_total, block_size, 2), jnp.int32)
        .at[buffer_index]
        .set(local_pattern, mode="drop")
    )
    recv_msgs, recv_pattern = (
        lax.all_to_all(send_msgs, "band", split_axis=0, concat_axis=0, tiled=True),
        lax.all_to_all(send_pattern, "band", split_axis=0, concat_axis=0, tiled=True),
    )
    recv_incidence = incidence_of(recv_pattern, block_size).reshape(
        bands, per_band, capacity, block_size, block_size
    )
    aggregate = jnp.einsum(
        "pmcgk,pmcgl->mkl",
        recv_incidence,
        recv_msgs.reshape(bands, per_band, capacity, block_size, width),
        preferred_element_type=jnp.float32,
    )
    agg_half = aggregate.reshape(per_band * block_size, width).astype(jnp.bfloat16)
    pre_hidden = jnp.dot(mesh_rows, w_self, preferred_element_type=jnp.float32) + jnp.dot(
        agg_half, w_agg, preferred_element_type=jnp.float32
    )
    hidden = jax.nn.silu(pre_hidden).astype(jnp.bfloat16)
    mesh_out = (
        mesh_rows.astype(jnp.float32) + jnp.dot(hidden, w_out, preferred_element_type=jnp.float32)
    ).astype(jnp.bfloat16)
    d_hidden = lax.dot_general(
        cot_rows, w_out, (((1,), (1,)), ((), ())), preferred_element_type=jnp.float32
    )
    d_pre_hidden = (d_hidden * silu_slope(pre_hidden)).astype(jnp.bfloat16)
    grad_mesh = (
        cot_rows.astype(jnp.float32)
        + lax.dot_general(
            d_pre_hidden, w_self, (((1,), (1,)), ((), ())), preferred_element_type=jnp.float32
        )
    ).astype(jnp.bfloat16)
    d_aggregate = lax.dot_general(
        d_pre_hidden, w_agg, (((1,), (1,)), ((), ())), preferred_element_type=jnp.float32
    ).astype(jnp.bfloat16)
    d_blocks = d_aggregate.reshape(per_band, block_size, width)
    slot_adjoint = jnp.einsum(
        "pmcgk,mkl->pmcgl", recv_incidence, d_blocks, preferred_element_type=jnp.float32
    )
    returned = lax.all_to_all(
        slot_adjoint.reshape(slot_total, block_size, width),
        "band",
        split_axis=0,
        concat_axis=0,
        tiled=True,
    )
    d_messages = returned[jnp.minimum(buffer_index, slot_total - 1)]
    d_messages = d_messages * live_flag.astype(jnp.float32)[:, None, None]
    d_pre_msg = (d_messages.reshape(block_count * block_size, width) * silu_slope(pre_msg)).astype(
        jnp.bfloat16
    )
    grad_grid = lax.dot_general(
        d_pre_msg, w_msg, (((1,), (1,)), ((), ())), preferred_element_type=jnp.float32
    ).astype(jnp.bfloat16)
    stacked = jnp.concatenate(
        [
            row_product(mesh_rows, d_pre_hidden),
            row_product(agg_half, d_pre_hidden),
            row_product(hidden, cot_rows),
            row_product(grid_rows, d_pre_msg),
        ],
        axis=0,
    )
    weight_grads = lax.psum_scatter(stacked, ("band", "dp"), scatter_dimension=0, tiled=True)
    return (mesh_out[None], grad_mesh[None], grad_grid[None], weight_grads)


def mm(left, right):
    return jnp.dot(left, right, preferred_element_type=F32)


def mm_t(left, right):
    return lax.dot_general(left, right, (((1,), (1,)), ((), ())), preferred_element_type=F32)


def logistic_of(value):
    return 0.5 + 0.5 * jnp.tanh(0.5 * value)


def fused(
    bands,
    tile,
    target_h,
    owner_h,
    live_h,
    pattern_h,
    grid_h,
    mesh_h,
    cot_h,
    wm_h,
    ws_h,
    wa_h,
    wo_h,
    mesh_out_h,
    grad_mesh_h,
    grad_grid_h,
    wg_h,
    mesh_out_v,
    grad_mesh_v,
    gg_v,
    wg_v,
    target_s,
    owner_s,
    live_s,
    pattern_t,
    grid_v,
    mesh_v,
    cot_v,
    wm_v,
    ws_v,
    wa_v,
    wo_v,
    hits,
    hits_t,
    grid_t,
    msgs,
    slope,
    part,
    part_send,
    part_recv,
    dagg_all,
    dpm,
    sums,
    send_a,
    recv_a,
    send_b,
    recv_b,
    send_c,
    recv_c,
    total_c,
    in_sem,
    grid_sem,
    out_sem,
    gg_sem,
    part_ss,
    part_rs,
    dagg_ss,
    dagg_rs,
    a_ss,
    a_rs,
    b_ss,
    b_rs,
    c_ss,
    c_rs,
):
    me = lax.axis_index("band")
    dp = lax.axis_index("dp")
    core = dp % 2
    column = dp // 2
    core_mate = dp + 1 - 2 * core
    x_mate = (dp + 2) % 4
    nodes, width = grid_v.shape
    block = mesh_v.shape[0]
    mesh_rows = hits.shape[0]
    tiles = nodes // tile
    half = width // 2
    blocks = nodes // block

    loads = [
        pltpu.make_async_copy(src, dst, in_sem.at[i])
        for i, (src, dst) in enumerate(
            (
                (target_h, target_s),
                (owner_h, owner_s),
                (live_h, live_s),
                (pattern_h, pattern_t),
                (wm_h, wm_v),
                (mesh_h, mesh_v),
                (cot_h, cot_v),
                (ws_h, ws_v),
                (wa_h, wa_v),
                (wo_h, wo_v),
            )
        )
    ]

    def grid_load(t):
        rows = pl.ds(t * tile, tile)
        return pltpu.make_async_copy(grid_h.at[rows], grid_v.at[rows], grid_sem.at[t])

    for load in loads[:5]:
        load.start()
    for t in range(tiles):
        grid_load(t).start()
    for load in loads[5:]:
        load.start()

    barrier = pltpu.get_barrier_semaphore()
    for rel in range(1, bands):
        pl.semaphore_signal(
            barrier, inc=1, device_id={"band": (me + rel) % bands}, device_id_type=MESH
        )
    pl.semaphore_signal(barrier, inc=1, device_id={"dp": core_mate}, device_id_type=MESH)
    pl.semaphore_signal(barrier, inc=1, device_id={"dp": x_mate}, device_id_type=MESH)

    for load in loads[:4]:
        load.wait()
    live = live_s[0]
    offsets = []
    for k in range(blocks):
        position = owner_s[target_s[k]]
        offsets.append(jnp.where(k < live, position * block, -2 * mesh_rows))
    row_ids = lax.broadcasted_iota(jnp.int32, (mesh_rows, block), 0)
    for k in range(blocks):
        cols = pl.ds(k * block, block)
        first = pattern_t[0:1, cols] + offsets[k]
        second = pattern_t[1:2, cols] + offsets[k]
        hits[:, cols] = (
            (row_ids == first).astype(F32) + (row_ids == second).astype(F32)
        ).astype(BF16)

    loads[4].wait()
    for t in range(tiles):
        grid_load(t).wait()

    def part_copy(h, rel):
        other = (me + rel) % bands
        return pltpu.make_async_remote_copy(
            src_ref=part_send.at[h, pl.ds(pl.multiple_of(other * block, block), block)],
            dst_ref=part_recv.at[h, rel - 1],
            send_sem=part_ss.at[h, rel - 1],
            recv_sem=part_rs.at[h, rel - 1],
            device_id={"band": other},
            device_id_type=MESH,
        )

    rels = (2, 1, 3)
    for h in range(2):
        cols = slice(h * half, (h + 1) * half)

        @pl.loop(0, tiles)
        def _(t):
            rows = pl.ds(pl.multiple_of(t * tile, tile), tile)
            pre = mm(grid_v[rows, :], wm_v[:, cols])
            gate = logistic_of(pre)
            msgs[h, rows, :] = (pre * gate).astype(BF16)
            slope[h, rows, :] = gate * (1.0 + pre * (1.0 - gate))

        partial = mm(hits[...], msgs[h])
        part[:, cols] = partial
        part_send[h] = partial.astype(BF16)
        if h == 0:
            pl.semaphore_wait(barrier, bands + 1)
        for rel in rels:
            part_copy(h, rel).start()

    for load in loads[5:]:
        load.wait()
    mesh_rows_v = mesh_v[...]
    cot_rows = cot_v[...]
    pre_self = mm(mesh_rows_v, ws_v[...])
    d_hidden = mm_t(cot_rows, wo_v[...])

    for t in range(tiles):
        hits_t[t * tile : (t + 1) * tile, :] = hits[:, t * tile : (t + 1) * tile].T
    for t in range(tiles):
        grid_t[:, t * tile : (t + 1) * tile] = grid_v[t * tile : (t + 1) * tile, :].T

    own = pl.ds(pl.multiple_of(me * block, block), block)
    agg_parts = []
    for h in range(2):
        total = part[own, h * half : (h + 1) * half]
        for rel in rels:
            part_copy(h, rel).wait_recv()
            total = total + part_recv[h, rel - 1].astype(F32)
        agg_parts.append(total.astype(BF16))
    agg = jnp.concatenate(agg_parts, axis=1)
    pre_hidden = pre_self + mm(agg, wa_v[...])
    gate = logistic_of(pre_hidden)
    hidden = (pre_hidden * gate).astype(BF16)
    dph = (d_hidden * (gate * (1.0 + pre_hidden * (1.0 - gate)))).astype(BF16)

    def dagg_copy(h, rel):
        return pltpu.make_async_remote_copy(
            src_ref=dagg_all.at[h, own],
            dst_ref=dagg_all.at[h, own],
            send_sem=dagg_ss.at[h, rel - 1],
            recv_sem=dagg_rs.at[h, rel - 1],
            device_id={"band": (me + rel) % bands},
            device_id_type=MESH,
        )

    for h in range(2):
        dagg_all[h, own, :] = mm_t(dph, wa_v[h * half : (h + 1) * half, :]).astype(BF16)
        for rel in rels:
            dagg_copy(h, rel).start()

    def a_copy(b, h):
        return pltpu.make_async_remote_copy(
            src_ref=send_a.at[b, h],
            dst_ref=recv_a.at[b, h],
            send_sem=a_ss.at[b, h],
            recv_sem=a_rs.at[b, h],
            device_id={"dp": core_mate},
            device_id_type=MESH,
        )

    def b_copy(b, h):
        return pltpu.make_async_remote_copy(
            src_ref=send_b.at[b, h],
            dst_ref=recv_b.at[b, h],
            send_sem=b_ss.at[b, h],
            recv_sem=b_rs.at[b, h],
            device_id={"dp": x_mate},
            device_id_type=MESH,
        )

    def c_copy(rel, h):
        other = (me + rel) % bands
        return pltpu.make_async_remote_copy(
            src_ref=send_c.at[other, h],
            dst_ref=recv_c.at[rel - 1, h],
            send_sem=c_ss.at[rel - 1, h],
            recv_sem=c_rs.at[rel - 1, h],
            device_id={"band": other},
            device_id_type=MESH,
        )

    share = width // 4

    def share_of(b, h, x, c):
        return sums[b, h, pl.ds(pl.multiple_of((x * 2 + c) * share, share), share), :]

    def step_a(b, h):
        for x in range(2):
            send_a[b, h, x] = share_of(b, h, x, 1 - core).astype(BF16)
        a_copy(b, h).start()

    def step_b(b, h):
        a_copy(b, h).wait_recv()
        away = 1 - column
        send_b[b, h] = (share_of(b, h, away, core) + recv_a[b, h, away].astype(F32)).astype(BF16)
        b_copy(b, h).start()

    def step_c(b, h):
        kept = share_of(b, h, column, core) + recv_a[b, h, column].astype(F32)
        b_copy(b, h).wait_recv()
        kept = kept + recv_b[b, h].astype(F32)
        total_c[b, h] = kept
        send_c[b, h] = kept.astype(BF16)

    def send_last(h, is_last):
        for rel in rels:
            other = (me + rel) % bands

            @pl.when((other == 3) if is_last else (other != 3))
            def _():
                c_copy(rel, h).start()

    halves = [slice(h * half, (h + 1) * half) for h in range(2)]
    for b, (left, right) in enumerate(((mesh_rows_v, dph), (agg, dph), (hidden, cot_rows))):
        for h in range(2):
            sums[b, h] = row_product(left, right[:, halves[h]])
            step_a(b, h)
    mesh_out_v[...] = (mesh_rows_v.astype(F32) + mm(hidden, wo_v[...])).astype(BF16)
    grad_mesh_v[...] = (cot_rows.astype(F32) + mm_t(dph, ws_v[...])).astype(BF16)
    stores = [
        pltpu.make_async_copy(mesh_out_v, mesh_out_h, out_sem.at[0]),
        pltpu.make_async_copy(grad_mesh_v, grad_mesh_h, out_sem.at[1]),
    ]
    for store in stores:
        store.start()
    for b in range(3):
        for h in range(2):
            step_b(b, h)

    for h in range(2):
        for rel in rels:
            dagg_copy(h, rel).wait_recv()

        @pl.loop(0, tiles)
        def _(t):
            rows = pl.ds(pl.multiple_of(t * tile, tile), tile)
            d_msg = mm(hits_t[rows, :], dagg_all[h])
            dpm[rows, halves[h]] = (d_msg * slope[h, rows, :]).astype(BF16)

        sums[3, h] = mm(grid_t[...], dpm[:, halves[h]])
        step_a(3, h)
        if h == 0:
            step_b(3, 0)
            for g in range(2):
                for b in range(3):
                    step_c(b, g)
                send_last(g, False)

    def gg_store(t):
        rows = pl.ds(pl.multiple_of(t * tile, tile), tile)
        return pltpu.make_async_copy(gg_v.at[rows], grad_grid_h.at[rows], gg_sem.at[t])

    def grid_grads(low, high):
        @pl.loop(low, high)
        def _(t):
            rows = pl.ds(pl.multiple_of(t * tile, tile), tile)
            gg_v[rows, :] = mm_t(dpm[rows, :], wm_v[...]).astype(BF16)
            gg_store(t).start()

    step_c(3, 0)
    send_last(0, True)
    step_b(3, 1)
    grid_grads(0, tiles // 2)
    step_c(3, 1)
    send_last(1, True)
    grid_grads(tiles // 2, tiles)

    for h in range(2):
        total = total_c[me, h]
        for rel in rels:
            c_copy(rel, h).wait_recv()
            total = total + recv_c[rel - 1, h].astype(F32)
        wg_v[:, halves[h]] = total
    stores.append(pltpu.make_async_copy(wg_v, wg_h, out_sem.at[2]))
    stores[2].start()

    @pl.loop(0, tiles)
    def _(t):
        gg_store(t).wait()

    for rel in rels:
        for h in range(2):
            part_copy(h, rel).wait_send()
            dagg_copy(h, rel).wait_send()
            c_copy(rel, h).wait_send()
    for b in range(4):
        for h in range(2):
            a_copy(b, h).wait_send()
            b_copy(b, h).wait_send()
    for store in stores:
        store.wait()


def store_all(*refs):
    count = len(refs) // 2
    sems = refs[-1]
    copies = [pltpu.make_async_copy(refs[i], refs[count + i], sems.at[i]) for i in range(count)]
    for copy in copies:
        copy.start()
    for copy in copies:
        copy.wait()


def fused_shards(
    grid_latent,
    mesh_latent,
    cotangent,
    w_msg,
    w_self,
    w_agg,
    w_out,
    target,
    owner_map,
    pattern,
    live_blocks,
):
    bands = lax.axis_size("band")
    nodes, width = grid_latent.shape[1:]
    block = mesh_latent.shape[1]
    rows = bands * block
    tile = 2 * block
    tiles = nodes // tile
    half = width // 2
    share = width // 4
    anywhere = pl.BlockSpec(memory_space=pl.ANY)
    hbm = pl.BlockSpec(memory_space=pltpu.HBM)
    dma = pltpu.SemaphoreType.DMA
    vmem = pltpu.VMEM
    shapes = (
        jax.ShapeDtypeStruct((block, width), BF16),
        jax.ShapeDtypeStruct((block, width), BF16),
        jax.ShapeDtypeStruct((nodes, width), BF16),
        jax.ShapeDtypeStruct((share, width), F32),
    )
    results = pl.pallas_call(
        functools.partial(fused, bands, tile),
        out_shape=shapes,
        in_specs=[hbm] * 11,
        out_specs=(anywhere,) * 4,
        scratch_shapes=[
            vmem((block, width), BF16),
            vmem((block, width), BF16),
            vmem((nodes, width), BF16),
            vmem((share, width), F32),
            pltpu.SMEM(target.shape[:1], jnp.int32),
            pltpu.SMEM(owner_map.shape, jnp.int32),
            pltpu.SMEM(live_blocks.shape, jnp.int32),
            vmem((2, nodes), jnp.int32),
            vmem((nodes, width), BF16),
            vmem((block, width), BF16),
            vmem((block, width), BF16),
            vmem((width, width), BF16),
            vmem((width, width), BF16),
            vmem((width, width), BF16),
            vmem((width, width), BF16),
            vmem((rows, nodes), BF16),
            vmem((nodes, rows), BF16),
            vmem((width, nodes), BF16),
            vmem((2, nodes, half), BF16),
            vmem((2, nodes, half), F32),
            vmem((rows, width), F32),
            vmem((2, rows, half), BF16),
            vmem((2, bands - 1, block, half), BF16),
            vmem((2, rows, half), BF16),
            vmem((nodes, width), BF16),
            vmem((4, 2, width, half), F32),
            vmem((4, 2, 2, share, half), BF16),
            vmem((4, 2, 2, share, half), BF16),
            vmem((4, 2, share, half), BF16),
            vmem((4, 2, share, half), BF16),
            vmem((4, 2, share, half), BF16),
            vmem((bands - 1, 2, share, half), BF16),
            vmem((4, 2, share, half), F32),
            dma((10,)),
            dma((tiles,)),
            dma((3,)),
            dma((tiles,)),
            dma((2, bands - 1)),
            dma((2, bands - 1)),
            dma((2, bands - 1)),
            dma((2, bands - 1)),
            dma((4, 2)),
            dma((4, 2)),
            dma((4, 2)),
            dma((4, 2)),
            dma((bands - 1, 2)),
            dma((bands - 1, 2)),
        ],
        compiler_params=pltpu.CompilerParams(
            collective_id=0, has_side_effects=True, vmem_limit_bytes=64 * 2**20
        ),
        name="encoder_step",
    )(
        target[:, 0],
        owner_map,
        live_blocks,
        pattern.T,
        grid_latent[0],
        mesh_latent[0],
        cotangent[0],
        w_msg,
        w_self,
        w_agg,
        w_out,
    )
    mesh_out, grad_mesh, grad_grid, weight_grads = pl.pallas_call(
        store_all,
        out_shape=shapes,
        in_specs=[anywhere] * 4,
        out_specs=(hbm,) * 4,
        scratch_shapes=[dma((4,))],
        compiler_params=pltpu.CompilerParams(vmem_limit_bytes=64 * 2**20),
        name="store_results",
    )(*results)
    return mesh_out[None], grad_mesh[None], grad_grid[None], weight_grads


def solution(mesh):
    in_specs = (
        P(("groups", "dp"), "band", None),
        P(("groups", "dp"), "band", None),
        P(("groups", "dp"), "band", None),
        P(),
        P(),
        P(),
        P(),
        P(("groups", "band"), None),
        P("groups"),
        P(("groups", "band"), None),
        P(("groups", "band")),
    )
    out_specs = (
        P(("groups", "dp"), "band", None),
        P(("groups", "dp"), "band", None),
        P(("groups", "dp"), "band", None),
        P(("groups", "band", "dp"), None),
    )
    body = fused_shards if mesh.shape["band"] == 4 and mesh.shape["dp"] == 4 else shards
    return jax.shard_map(body, mesh=mesh, in_specs=in_specs, out_specs=out_specs, check_vma=False)
```

```python
import functools
import jax
import jax.numpy as jnp
from jax import lax
from jax.experimental import pallas as pl
from jax.experimental.pallas import tpu as pltpu
from jax.sharding import PartitionSpec as P

MESH = pl.DeviceIdType.MESH
F32 = jnp.float32
BF16 = jnp.bfloat16


def silu_slope(value):
    logistic = jax.nn.sigmoid(value)
    return logistic * (1.0 + value * (1.0 - logistic))


def incidence_of(edge_pattern, block_size):
    columns = jnp.arange(block_size, dtype=jnp.int32)
    first_hit = (edge_pattern[..., 0:1] == columns).astype(jnp.bfloat16)
    second_hit = (edge_pattern[..., 1:2] == columns).astype(jnp.bfloat16)
    return first_hit + second_hit


def row_product(left, right):
    return lax.dot_general(
        left, right, (((0,), (0,)), ((), ())), preferred_element_type=jnp.float32
    )


def shards(
    grid_latent,
    mesh_latent,
    cotangent,
    w_msg,
    w_self,
    w_agg,
    w_out,
    target,
    owner_map,
    pattern,
    live_blocks,
):
    grid_rows = grid_latent[0]
    mesh_rows = mesh_latent[0]
    cot_rows = cotangent[0]
    block_count = target.shape[0]
    width = grid_rows.shape[1]
    block_size = grid_rows.shape[0] // block_count
    bands = lax.axis_size("band")
    mesh_blocks = owner_map.shape[0]
    per_band = mesh_blocks // bands
    capacity = (block_count + mesh_blocks - 1) // mesh_blocks
    slot_total = mesh_blocks * capacity
    block_ids = jnp.arange(block_count, dtype=jnp.int32)
    live_flag = block_ids < live_blocks[0]
    matches = target[:, 0][:, None] == jnp.arange(mesh_blocks, dtype=jnp.int32)[None, :]
    mesh_slot = jnp.sum(jnp.where(matches, owner_map[None, :], 0), axis=1)
    same_slot = (
        (mesh_slot[:, None] == mesh_slot[None, :])
        & live_flag[None, :]
        & (block_ids[None, :] < block_ids[:, None])
    )
    slot_rank = jnp.sum(same_slot.astype(jnp.int32), axis=1)
    buffer_index = jnp.where(live_flag, mesh_slot * capacity + slot_rank, slot_total)
    pre_msg = jnp.dot(grid_rows, w_msg, preferred_element_type=jnp.float32)
    messages = jax.nn.silu(pre_msg).astype(jnp.bfloat16).reshape(block_count, block_size, width)
    local_pattern = pattern.reshape(block_count, block_size, 2)
    send_msgs = (
        jnp.zeros((slot_total, block_size, width), jnp.bfloat16)
        .at[buffer_index]
        .set(messages, mode="drop")
    )
    send_pattern = (
        jnp.zeros((slot_total, block_size, 2), jnp.int32)
        .at[buffer_index]
        .set(local_pattern, mode="drop")
    )
    recv_msgs, recv_pattern = (
        lax.all_to_all(send_msgs, "band", split_axis=0, concat_axis=0, tiled=True),
        lax.all_to_all(send_pattern, "band", split_axis=0, concat_axis=0, tiled=True),
    )
    recv_incidence = incidence_of(recv_pattern, block_size).reshape(
        bands, per_band, capacity, block_size, block_size
    )
    aggregate = jnp.einsum(
        "pmcgk,pmcgl->mkl",
        recv_incidence,
        recv_msgs.reshape(bands, per_band, capacity, block_size, width),
        preferred_element_type=jnp.float32,
    )
    agg_half = aggregate.reshape(per_band * block_size, width).astype(jnp.bfloat16)
    pre_hidden = jnp.dot(mesh_rows, w_self, preferred_element_type=jnp.float32) + jnp.dot(
        agg_half, w_agg, preferred_element_type=jnp.float32
    )
    hidden = jax.nn.silu(pre_hidden).astype(jnp.bfloat16)
    mesh_out = (
        mesh_rows.astype(jnp.float32) + jnp.dot(hidden, w_out, preferred_element_type=jnp.float32)
    ).astype(jnp.bfloat16)
    d_hidden = lax.dot_general(
        cot_rows, w_out, (((1,), (1,)), ((), ())), preferred_element_type=jnp.float32
    )
    d_pre_hidden = (d_hidden * silu_slope(pre_hidden)).astype(jnp.bfloat16)
    grad_mesh = (
        cot_rows.astype(jnp.float32)
        + lax.dot_general(
            d_pre_hidden, w_self, (((1,), (1,)), ((), ())), preferred_element_type=jnp.float32
        )
    ).astype(jnp.bfloat16)
    d_aggregate = lax.dot_general(
        d_pre_hidden, w_agg, (((1,), (1,)), ((), ())), preferred_element_type=jnp.float32
    ).astype(jnp.bfloat16)
    d_blocks = d_aggregate.reshape(per_band, block_size, width)
    slot_adjoint = jnp.einsum(
        "pmcgk,mkl->pmcgl", recv_incidence, d_blocks, preferred_element_type=jnp.float32
    )
    returned = lax.all_to_all(
        slot_adjoint.reshape(slot_total, block_size, width),
        "band",
        split_axis=0,
        concat_axis=0,
        tiled=True,
    )
    d_messages = returned[jnp.minimum(buffer_index, slot_total - 1)]
    d_messages = d_messages * live_flag.astype(jnp.float32)[:, None, None]
    d_pre_msg = (d_messages.reshape(block_count * block_size, width) * silu_slope(pre_msg)).astype(
        jnp.bfloat16
    )
    grad_grid = lax.dot_general(
        d_pre_msg, w_msg, (((1,), (1,)), ((), ())), preferred_element_type=jnp.float32
    ).astype(jnp.bfloat16)
    stacked = jnp.concatenate(
        [
            row_product(mesh_rows, d_pre_hidden),
            row_product(agg_half, d_pre_hidden),
            row_product(hidden, cot_rows),
            row_product(grid_rows, d_pre_msg),
        ],
        axis=0,
    )
    weight_grads = lax.psum_scatter(stacked, ("band", "dp"), scatter_dimension=0, tiled=True)
    return (mesh_out[None], grad_mesh[None], grad_grid[None], weight_grads)


def mm(left, right):
    return jnp.dot(left, right, preferred_element_type=F32)


def mm_t(left, right):
    return lax.dot_general(left, right, (((1,), (1,)), ((), ())), preferred_element_type=F32)


def logistic_of(value):
    return 0.5 + 0.5 * jnp.tanh(0.5 * value)


def fused(
    bands,
    tile,
    target_h,
    owner_h,
    live_h,
    pattern_h,
    grid_h,
    mesh_h,
    cot_h,
    wm_h,
    ws_h,
    wa_h,
    wo_h,
    mesh_out_h,
    grad_mesh_h,
    grad_grid_h,
    wg_h,
    mesh_out_v,
    grad_mesh_v,
    gg_v,
    wg_v,
    target_s,
    owner_s,
    live_s,
    pattern_t,
    grid_v,
    mesh_v,
    cot_v,
    wm_v,
    ws_v,
    wa_v,
    wo_v,
    hits,
    hits_t,
    grid_t,
    msgs,
    slope,
    part,
    part_send,
    part_recv,
    dagg_all,
    dpm,
    sums,
    send_a,
    recv_a,
    send_b,
    recv_b,
    send_c,
    recv_c,
    total_c,
    in_sem,
    grid_sem,
    out_sem,
    gg_sem,
    part_ss,
    part_rs,
    dagg_ss,
    dagg_rs,
    a_ss,
    a_rs,
    b_ss,
    b_rs,
    c_ss,
    c_rs,
):
    me = lax.axis_index("band")
    dp = lax.axis_index("dp")
    core = dp % 2
    column = dp // 2
    core_mate = dp + 1 - 2 * core
    x_mate = (dp + 2) % 4
    nodes, width = grid_v.shape
    block = mesh_v.shape[0]
    mesh_rows = hits.shape[0]
    tiles = nodes // tile
    half = width // 2
    blocks = nodes // block

    loads = [
        pltpu.make_async_copy(src, dst, in_sem.at[i])
        for i, (src, dst) in enumerate(
            (
                (target_h, target_s),
                (owner_h, owner_s),
                (live_h, live_s),
                (pattern_h, pattern_t),
                (wm_h, wm_v),
                (mesh_h, mesh_v),
                (cot_h, cot_v),
                (ws_h, ws_v),
                (wa_h, wa_v),
                (wo_h, wo_v),
            )
        )
    ]

    def grid_load(t):
        rows = pl.ds(t * tile, tile)
        return pltpu.make_async_copy(grid_h.at[rows], grid_v.at[rows], grid_sem.at[t])

    for load in loads[:5]:
        load.start()
    for t in range(tiles):
        grid_load(t).start()
    for load in loads[5:]:
        load.start()

    barrier = pltpu.get_barrier_semaphore()
    for rel in range(1, bands):
        pl.semaphore_signal(
            barrier, inc=1, device_id={"band": (me + rel) % bands}, device_id_type=MESH
        )
    pl.semaphore_signal(barrier, inc=1, device_id={"dp": core_mate}, device_id_type=MESH)
    pl.semaphore_signal(barrier, inc=1, device_id={"dp": x_mate}, device_id_type=MESH)

    for load in loads[:4]:
        load.wait()
    live = live_s[0]
    offsets = []
    for k in range(blocks):
        position = owner_s[target_s[k]]
        offsets.append(jnp.where(k < live, position * block, -2 * mesh_rows))
    row_ids = lax.broadcasted_iota(jnp.int32, (mesh_rows, block), 0)
    for k in range(blocks):
        cols = pl.ds(k * block, block)
        first = pattern_t[0:1, cols] + offsets[k]
        second = pattern_t[1:2, cols] + offsets[k]
        hits[:, cols] = (
            (row_ids == first).astype(F32) + (row_ids == second).astype(F32)
        ).astype(BF16)

    loads[4].wait()
    for t in range(tiles):
        grid_load(t).wait()

    def part_copy(h, rel):
        other = (me + rel) % bands
        return pltpu.make_async_remote_copy(
            src_ref=part_send.at[h, pl.ds(pl.multiple_of(other * block, block), block)],
            dst_ref=part_recv.at[h, rel - 1],
            send_sem=part_ss.at[h, rel - 1],
            recv_sem=part_rs.at[h, rel - 1],
            device_id={"band": other},
            device_id_type=MESH,
        )

    rels = (2, 1, 3)
    for h in range(2):
        cols = slice(h * half, (h + 1) * half)

        @pl.loop(0, tiles)
        def _(t):
            rows = pl.ds(pl.multiple_of(t * tile, tile), tile)
            pre = mm(grid_v[rows, :], wm_v[:, cols])
            gate = logistic_of(pre)
            msgs[h, rows, :] = (pre * gate).astype(BF16)
            slope[h, rows, :] = gate * (1.0 + pre * (1.0 - gate))

        partial = mm(hits[...], msgs[h])
        part[:, cols] = partial
        part_send[h] = partial.astype(BF16)
        if h == 0:
            pl.semaphore_wait(barrier, bands + 1)
        for rel in rels:
            part_copy(h, rel).start()

    for load in loads[5:]:
        load.wait()
    mesh_rows_v = mesh_v[...]
    cot_rows = cot_v[...]
    pre_self = mm(mesh_rows_v, ws_v[...])
    d_hidden = mm_t(cot_rows, wo_v[...])

    for t in range(tiles):
        hits_t[t * tile : (t + 1) * tile, :] = hits[:, t * tile : (t + 1) * tile].T
    for t in range(tiles):
        grid_t[:, t * tile : (t + 1) * tile] = grid_v[t * tile : (t + 1) * tile, :].T

    own = pl.ds(pl.multiple_of(me * block, block), block)
    agg_parts = []
    for h in range(2):
        total = part[own, h * half : (h + 1) * half]
        for rel in rels:
            part_copy(h, rel).wait_recv()
            total = total + part_recv[h, rel - 1].astype(F32)
        agg_parts.append(total.astype(BF16))
    agg = jnp.concatenate(agg_parts, axis=1)
    pre_hidden = pre_self + mm(agg, wa_v[...])
    gate = logistic_of(pre_hidden)
    hidden = (pre_hidden * gate).astype(BF16)
    dph = (d_hidden * (gate * (1.0 + pre_hidden * (1.0 - gate)))).astype(BF16)

    def dagg_copy(h, rel):
        return pltpu.make_async_remote_copy(
            src_ref=dagg_all.at[h, own],
            dst_ref=dagg_all.at[h, own],
            send_sem=dagg_ss.at[h, rel - 1],
            recv_sem=dagg_rs.at[h, rel - 1],
            device_id={"band": (me + rel) % bands},
            device_id_type=MESH,
        )

    for h in range(2):
        dagg_all[h, own, :] = mm_t(dph, wa_v[h * half : (h + 1) * half, :]).astype(BF16)
        for rel in rels:
            dagg_copy(h, rel).start()

    def a_copy(b, h):
        return pltpu.make_async_remote_copy(
            src_ref=send_a.at[b, h],
            dst_ref=recv_a.at[b, h],
            send_sem=a_ss.at[b, h],
            recv_sem=a_rs.at[b, h],
            device_id={"dp": core_mate},
            device_id_type=MESH,
        )

    def b_copy(b, h):
        return pltpu.make_async_remote_copy(
            src_ref=send_b.at[b, h],
            dst_ref=recv_b.at[b, h],
            send_sem=b_ss.at[b, h],
            recv_sem=b_rs.at[b, h],
            device_id={"dp": x_mate},
            device_id_type=MESH,
        )

    def c_copy(rel, h):
        other = (me + rel) % bands
        return pltpu.make_async_remote_copy(
            src_ref=send_c.at[other, h],
            dst_ref=recv_c.at[rel - 1, h],
            send_sem=c_ss.at[rel - 1, h],
            recv_sem=c_rs.at[rel - 1, h],
            device_id={"band": other},
            device_id_type=MESH,
        )

    share = width // 4

    def share_of(b, h, x, c):
        return sums[b, h, pl.ds(pl.multiple_of((x * 2 + c) * share, share), share), :]

    def step_a(b, h):
        for x in range(2):
            send_a[b, h, x] = share_of(b, h, x, 1 - core).astype(BF16)
        a_copy(b, h).start()

    def step_b(b, h):
        a_copy(b, h).wait_recv()
        away = 1 - column
        send_b[b, h] = (share_of(b, h, away, core) + recv_a[b, h, away].astype(F32)).astype(BF16)
        b_copy(b, h).start()

    def step_c(b, h):
        kept = share_of(b, h, column, core) + recv_a[b, h, column].astype(F32)
        b_copy(b, h).wait_recv()
        kept = kept + recv_b[b, h].astype(F32)
        total_c[b, h] = kept
        send_c[b, h] = kept.astype(BF16)

    def send_last(h, is_last):
        for rel in rels:
            other = (me + rel) % bands

            @pl.when((other == 3) if is_last else (other != 3))
            def _():
                c_copy(rel, h).start()

    halves = [slice(h * half, (h + 1) * half) for h in range(2)]
    for b, (left, right) in enumerate(((mesh_rows_v, dph), (agg, dph), (hidden, cot_rows))):
        for h in range(2):
            sums[b, h] = row_product(left, right[:, halves[h]])
            step_a(b, h)
    mesh_out_v[...] = (mesh_rows_v.astype(F32) + mm(hidden, wo_v[...])).astype(BF16)
    grad_mesh_v[...] = (cot_rows.astype(F32) + mm_t(dph, ws_v[...])).astype(BF16)
    stores = [
        pltpu.make_async_copy(mesh_out_v, mesh_out_h, out_sem.at[0]),
        pltpu.make_async_copy(grad_mesh_v, grad_mesh_h, out_sem.at[1]),
    ]
    for store in stores:
        store.start()
    for b in range(3):
        for h in range(2):
            step_b(b, h)

    for h in range(2):
        for rel in rels:
            dagg_copy(h, rel).wait_recv()

        @pl.loop(0, tiles)
        def _(t):
            rows = pl.ds(pl.multiple_of(t * tile, tile), tile)
            d_msg = mm(hits_t[rows, :], dagg_all[h])
            dpm[rows, halves[h]] = (d_msg * slope[h, rows, :]).astype(BF16)

        sums[3, h] = mm(grid_t[...], dpm[:, halves[h]])
        step_a(3, h)
        if h == 0:
            step_b(3, 0)
            for g in range(2):
                for b in range(3):
                    step_c(b, g)
                send_last(g, False)

    def gg_store(t):
        rows = pl.ds(pl.multiple_of(t * tile, tile), tile)
        return pltpu.make_async_copy(gg_v.at[rows], grad_grid_h.at[rows], gg_sem.at[t])

    def grid_grads(low, high):
        @pl.loop(low, high)
        def _(t):
            rows = pl.ds(pl.multiple_of(t * tile, tile), tile)
            gg_v[rows, :] = mm_t(dpm[rows, :], wm_v[...]).astype(BF16)
            gg_store(t).start()

    step_c(3, 0)
    send_last(0, True)
    step_b(3, 1)
    grid_grads(0, tiles // 2)
    step_c(3, 1)
    send_last(1, True)
    grid_grads(tiles // 2, tiles)

    for h in range(2):
        total = total_c[me, h]
        for rel in rels:
            c_copy(rel, h).wait_recv()
            total = total + recv_c[rel - 1, h].astype(F32)
        wg_v[:, halves[h]] = total
    stores.append(pltpu.make_async_copy(wg_v, wg_h, out_sem.at[2]))
    stores[2].start()

    @pl.loop(0, tiles)
    def _(t):
        gg_store(t).wait()

    for rel in rels:
        for h in range(2):
            part_copy(h, rel).wait_send()
            dagg_copy(h, rel).wait_send()
            c_copy(rel, h).wait_send()
    for b in range(4):
        for h in range(2):
            a_copy(b, h).wait_send()
            b_copy(b, h).wait_send()
    for store in stores:
        store.wait()


def store_all(chunk, *refs):
    sources, targets, stages, sems = refs[:4], refs[4:8], refs[8:12], refs[12]
    pairs = []
    for source, target, stage in zip(sources, targets, stages):
        for low in range(0, source.shape[0], chunk):
            rows = pl.ds(low, min(chunk, source.shape[0]))
            sem = sems.at[len(pairs)]
            pairs.append(
                (
                    pltpu.make_async_copy(source.at[rows], stage.at[rows], sem),
                    pltpu.make_async_copy(stage.at[rows], target.at[rows], sem),
                )
            )
    for load, _ in pairs:
        load.start()
    for load, store in pairs:
        load.wait()
        store.start()
    for _, store in pairs:
        store.wait()


def fused_shards(
    grid_latent,
    mesh_latent,
    cotangent,
    w_msg,
    w_self,
    w_agg,
    w_out,
    target,
    owner_map,
    pattern,
    live_blocks,
):
    bands = lax.axis_size("band")
    nodes, width = grid_latent.shape[1:]
    block = mesh_latent.shape[1]
    rows = bands * block
    tile = 2 * block
    tiles = nodes // tile
    half = width // 2
    share = width // 4
    anywhere = pl.BlockSpec(memory_space=pl.ANY)
    hbm = pl.BlockSpec(memory_space=pltpu.HBM)
    dma = pltpu.SemaphoreType.DMA
    vmem = pltpu.VMEM
    shapes = (
        jax.ShapeDtypeStruct((block, width), BF16),
        jax.ShapeDtypeStruct((block, width), BF16),
        jax.ShapeDtypeStruct((nodes, width), BF16),
        jax.ShapeDtypeStruct((share, width), F32),
    )
    results = pl.pallas_call(
        functools.partial(fused, bands, tile),
        out_shape=shapes,
        in_specs=[hbm] * 11,
        out_specs=(anywhere,) * 4,
        scratch_shapes=[
            vmem((block, width), BF16),
            vmem((block, width), BF16),
            vmem((nodes, width), BF16),
            vmem((share, width), F32),
            pltpu.SMEM(target.shape[:1], jnp.int32),
            pltpu.SMEM(owner_map.shape, jnp.int32),
            pltpu.SMEM(live_blocks.shape, jnp.int32),
            vmem((2, nodes), jnp.int32),
            vmem((nodes, width), BF16),
            vmem((block, width), BF16),
            vmem((block, width), BF16),
            vmem((width, width), BF16),
            vmem((width, width), BF16),
            vmem((width, width), BF16),
            vmem((width, width), BF16),
            vmem((rows, nodes), BF16),
            vmem((nodes, rows), BF16),
            vmem((width, nodes), BF16),
            vmem((2, nodes, half), BF16),
            vmem((2, nodes, half), F32),
            vmem((rows, width), F32),
            vmem((2, rows, half), BF16),
            vmem((2, bands - 1, block, half), BF16),
            vmem((2, rows, half), BF16),
            vmem((nodes, width), BF16),
            vmem((4, 2, width, half), F32),
            vmem((4, 2, 2, share, half), BF16),
            vmem((4, 2, 2, share, half), BF16),
            vmem((4, 2, share, half), BF16),
            vmem((4, 2, share, half), BF16),
            vmem((4, 2, share, half), BF16),
            vmem((bands - 1, 2, share, half), BF16),
            vmem((4, 2, share, half), F32),
            dma((10,)),
            dma((tiles,)),
            dma((3,)),
            dma((tiles,)),
            dma((2, bands - 1)),
            dma((2, bands - 1)),
            dma((2, bands - 1)),
            dma((2, bands - 1)),
            dma((4, 2)),
            dma((4, 2)),
            dma((4, 2)),
            dma((4, 2)),
            dma((bands - 1, 2)),
            dma((bands - 1, 2)),
        ],
        compiler_params=pltpu.CompilerParams(
            collective_id=0, has_side_effects=True, vmem_limit_bytes=64 * 2**20
        ),
        name="encoder_step",
    )(
        target[:, 0],
        owner_map,
        live_blocks,
        pattern.T,
        grid_latent[0],
        mesh_latent[0],
        cotangent[0],
        w_msg,
        w_self,
        w_agg,
        w_out,
    )
    chunk = 2 * tile
    mesh_out, grad_mesh, grad_grid, weight_grads = pl.pallas_call(
        functools.partial(store_all, chunk),
        out_shape=shapes,
        in_specs=[anywhere] * 4,
        out_specs=(hbm,) * 4,
        scratch_shapes=[vmem(shape.shape, shape.dtype) for shape in shapes]
        + [dma((3 + nodes // chunk,))],
        compiler_params=pltpu.CompilerParams(vmem_limit_bytes=64 * 2**20),
        name="store_results",
    )(*results)
    return mesh_out[None], grad_mesh[None], grad_grid[None], weight_grads


def solution(mesh):
    in_specs = (
        P(("groups", "dp"), "band", None),
        P(("groups", "dp"), "band", None),
        P(("groups", "dp"), "band", None),
        P(),
        P(),
        P(),
        P(),
        P(("groups", "band"), None),
        P("groups"),
        P(("groups", "band"), None),
        P(("groups", "band")),
    )
    out_specs = (
        P(("groups", "dp"), "band", None),
        P(("groups", "dp"), "band", None),
        P(("groups", "dp"), "band", None),
        P(("groups", "band", "dp"), None),
    )
    body = fused_shards if mesh.shape["band"] == 4 and mesh.shape["dp"] == 4 else shards
    return jax.shard_map(body, mesh=mesh, in_specs=in_specs, out_specs=out_specs, check_vma=False)
```

```python
import functools
import jax
import jax.numpy as jnp
from jax import lax
from jax.experimental import pallas as pl
from jax.experimental.pallas import tpu as pltpu
from jax.sharding import PartitionSpec as P

MESH = pl.DeviceIdType.MESH
F32 = jnp.float32
BF16 = jnp.bfloat16


def silu_slope(value):
    logistic = jax.nn.sigmoid(value)
    return logistic * (1.0 + value * (1.0 - logistic))


def incidence_of(edge_pattern, block_size):
    columns = jnp.arange(block_size, dtype=jnp.int32)
    first_hit = (edge_pattern[..., 0:1] == columns).astype(jnp.bfloat16)
    second_hit = (edge_pattern[..., 1:2] == columns).astype(jnp.bfloat16)
    return first_hit + second_hit


def row_product(left, right):
    return lax.dot_general(
        left, right, (((0,), (0,)), ((), ())), preferred_element_type=jnp.float32
    )


def shards(
    grid_latent,
    mesh_latent,
    cotangent,
    w_msg,
    w_self,
    w_agg,
    w_out,
    target,
    owner_map,
    pattern,
    live_blocks,
):
    grid_rows = grid_latent[0]
    mesh_rows = mesh_latent[0]
    cot_rows = cotangent[0]
    block_count = target.shape[0]
    width = grid_rows.shape[1]
    block_size = grid_rows.shape[0] // block_count
    bands = lax.axis_size("band")
    mesh_blocks = owner_map.shape[0]
    per_band = mesh_blocks // bands
    capacity = (block_count + mesh_blocks - 1) // mesh_blocks
    slot_total = mesh_blocks * capacity
    block_ids = jnp.arange(block_count, dtype=jnp.int32)
    live_flag = block_ids < live_blocks[0]
    matches = target[:, 0][:, None] == jnp.arange(mesh_blocks, dtype=jnp.int32)[None, :]
    mesh_slot = jnp.sum(jnp.where(matches, owner_map[None, :], 0), axis=1)
    same_slot = (
        (mesh_slot[:, None] == mesh_slot[None, :])
        & live_flag[None, :]
        & (block_ids[None, :] < block_ids[:, None])
    )
    slot_rank = jnp.sum(same_slot.astype(jnp.int32), axis=1)
    buffer_index = jnp.where(live_flag, mesh_slot * capacity + slot_rank, slot_total)
    pre_msg = jnp.dot(grid_rows, w_msg, preferred_element_type=jnp.float32)
    messages = jax.nn.silu(pre_msg).astype(jnp.bfloat16).reshape(block_count, block_size, width)
    local_pattern = pattern.reshape(block_count, block_size, 2)
    send_msgs = (
        jnp.zeros((slot_total, block_size, width), jnp.bfloat16)
        .at[buffer_index]
        .set(messages, mode="drop")
    )
    send_pattern = (
        jnp.zeros((slot_total, block_size, 2), jnp.int32)
        .at[buffer_index]
        .set(local_pattern, mode="drop")
    )
    recv_msgs, recv_pattern = (
        lax.all_to_all(send_msgs, "band", split_axis=0, concat_axis=0, tiled=True),
        lax.all_to_all(send_pattern, "band", split_axis=0, concat_axis=0, tiled=True),
    )
    recv_incidence = incidence_of(recv_pattern, block_size).reshape(
        bands, per_band, capacity, block_size, block_size
    )
    aggregate = jnp.einsum(
        "pmcgk,pmcgl->mkl",
        recv_incidence,
        recv_msgs.reshape(bands, per_band, capacity, block_size, width),
        preferred_element_type=jnp.float32,
    )
    agg_half = aggregate.reshape(per_band * block_size, width).astype(jnp.bfloat16)
    pre_hidden = jnp.dot(mesh_rows, w_self, preferred_element_type=jnp.float32) + jnp.dot(
        agg_half, w_agg, preferred_element_type=jnp.float32
    )
    hidden = jax.nn.silu(pre_hidden).astype(jnp.bfloat16)
    mesh_out = (
        mesh_rows.astype(jnp.float32) + jnp.dot(hidden, w_out, preferred_element_type=jnp.float32)
    ).astype(jnp.bfloat16)
    d_hidden = lax.dot_general(
        cot_rows, w_out, (((1,), (1,)), ((), ())), preferred_element_type=jnp.float32
    )
    d_pre_hidden = (d_hidden * silu_slope(pre_hidden)).astype(jnp.bfloat16)
    grad_mesh = (
        cot_rows.astype(jnp.float32)
        + lax.dot_general(
            d_pre_hidden, w_self, (((1,), (1,)), ((), ())), preferred_element_type=jnp.float32
        )
    ).astype(jnp.bfloat16)
    d_aggregate = lax.dot_general(
        d_pre_hidden, w_agg, (((1,), (1,)), ((), ())), preferred_element_type=jnp.float32
    ).astype(jnp.bfloat16)
    d_blocks = d_aggregate.reshape(per_band, block_size, width)
    slot_adjoint = jnp.einsum(
        "pmcgk,mkl->pmcgl", recv_incidence, d_blocks, preferred_element_type=jnp.float32
    )
    returned = lax.all_to_all(
        slot_adjoint.reshape(slot_total, block_size, width),
        "band",
        split_axis=0,
        concat_axis=0,
        tiled=True,
    )
    d_messages = returned[jnp.minimum(buffer_index, slot_total - 1)]
    d_messages = d_messages * live_flag.astype(jnp.float32)[:, None, None]
    d_pre_msg = (d_messages.reshape(block_count * block_size, width) * silu_slope(pre_msg)).astype(
        jnp.bfloat16
    )
    grad_grid = lax.dot_general(
        d_pre_msg, w_msg, (((1,), (1,)), ((), ())), preferred_element_type=jnp.float32
    ).astype(jnp.bfloat16)
    stacked = jnp.concatenate(
        [
            row_product(mesh_rows, d_pre_hidden),
            row_product(agg_half, d_pre_hidden),
            row_product(hidden, cot_rows),
            row_product(grid_rows, d_pre_msg),
        ],
        axis=0,
    )
    weight_grads = lax.psum_scatter(stacked, ("band", "dp"), scatter_dimension=0, tiled=True)
    return (mesh_out[None], grad_mesh[None], grad_grid[None], weight_grads)


def mm(left, right):
    return jnp.dot(left, right, preferred_element_type=F32)


def mm_t(left, right):
    return lax.dot_general(left, right, (((1,), (1,)), ((), ())), preferred_element_type=F32)


def logistic_of(value):
    return 0.5 + 0.5 * jnp.tanh(0.5 * value)


def fused(
    bands,
    tile,
    target_h,
    owner_h,
    live_h,
    pattern_h,
    grid_h,
    mesh_h,
    cot_h,
    wm_h,
    ws_h,
    wa_h,
    wo_h,
    mesh_out_h,
    grad_mesh_h,
    grad_grid_h,
    wg_h,
    mesh_out_v,
    grad_mesh_v,
    gg_v,
    wg_v,
    target_s,
    owner_s,
    live_s,
    pattern_t,
    grid_v,
    mesh_v,
    cot_v,
    wm_v,
    ws_v,
    wa_v,
    wo_v,
    hits,
    hits_t,
    grid_t,
    msgs,
    slope,
    part,
    part_send,
    part_recv,
    dagg_all,
    dpm,
    sums,
    send_a,
    recv_a,
    send_b,
    recv_b,
    send_c,
    recv_c,
    total_c,
    in_sem,
    grid_sem,
    out_sem,
    gg_sem,
    part_ss,
    part_rs,
    dagg_ss,
    dagg_rs,
    a_ss,
    a_rs,
    b_ss,
    b_rs,
    c_ss,
    c_rs,
):
    me = lax.axis_index("band")
    dp = lax.axis_index("dp")
    core = dp % 2
    column = dp // 2
    core_mate = dp + 1 - 2 * core
    x_mate = (dp + 2) % 4
    nodes, width = grid_v.shape
    block = mesh_v.shape[0]
    mesh_rows = hits.shape[0]
    tiles = nodes // tile
    half = width // 2
    blocks = nodes // block

    loads = [
        pltpu.make_async_copy(src, dst, in_sem.at[i])
        for i, (src, dst) in enumerate(
            (
                (target_h, target_s),
                (owner_h, owner_s),
                (live_h, live_s),
                (pattern_h, pattern_t),
                (wm_h, wm_v),
                (mesh_h, mesh_v),
                (cot_h, cot_v),
                (ws_h, ws_v),
                (wa_h, wa_v),
                (wo_h, wo_v),
            )
        )
    ]

    def grid_load(t):
        rows = pl.ds(t * tile, tile)
        return pltpu.make_async_copy(grid_h.at[rows], grid_v.at[rows], grid_sem.at[t])

    for load in loads[:5]:
        load.start()
    for t in range(tiles):
        grid_load(t).start()
    for load in loads[5:]:
        load.start()

    barrier = pltpu.get_barrier_semaphore()
    for rel in range(1, bands):
        pl.semaphore_signal(
            barrier, inc=1, device_id={"band": (me + rel) % bands}, device_id_type=MESH
        )
    pl.semaphore_signal(barrier, inc=1, device_id={"dp": core_mate}, device_id_type=MESH)
    pl.semaphore_signal(barrier, inc=1, device_id={"dp": x_mate}, device_id_type=MESH)

    for load in loads[:4]:
        load.wait()
    live = live_s[0]
    offsets = []
    for k in range(blocks):
        position = owner_s[target_s[k]]
        offsets.append(jnp.where(k < live, position * block, -2 * mesh_rows))
    row_ids = lax.broadcasted_iota(jnp.int32, (mesh_rows, block), 0)
    for k in range(blocks):
        cols = pl.ds(k * block, block)
        first = pattern_t[0:1, cols] + offsets[k]
        second = pattern_t[1:2, cols] + offsets[k]
        hits[:, cols] = (
            (row_ids == first).astype(F32) + (row_ids == second).astype(F32)
        ).astype(BF16)

    loads[4].wait()
    for t in range(tiles):
        grid_load(t).wait()

    def part_copy(h, rel):
        other = (me + rel) % bands
        return pltpu.make_async_remote_copy(
            src_ref=part_send.at[h, pl.ds(pl.multiple_of(other * block, block), block)],
            dst_ref=part_recv.at[h, rel - 1],
            send_sem=part_ss.at[h, rel - 1],
            recv_sem=part_rs.at[h, rel - 1],
            device_id={"band": other},
            device_id_type=MESH,
        )

    rels = (2, 1, 3)
    for h in range(2):
        cols = slice(h * half, (h + 1) * half)

        @pl.loop(0, tiles)
        def _(t):
            rows = pl.ds(pl.multiple_of(t * tile, tile), tile)
            pre = mm(grid_v[rows, :], wm_v[:, cols])
            gate = logistic_of(pre)
            msgs[h, rows, :] = (pre * gate).astype(BF16)
            slope[h, rows, :] = gate * (1.0 + pre * (1.0 - gate))

        partial = mm(hits[...], msgs[h])
        part[:, cols] = partial
        part_send[h] = partial.astype(BF16)
        if h == 0:
            pl.semaphore_wait(barrier, bands + 1)
        for rel in rels:
            part_copy(h, rel).start()

    for load in loads[5:]:
        load.wait()
    mesh_rows_v = mesh_v[...]
    cot_rows = cot_v[...]
    pre_self = mm(mesh_rows_v, ws_v[...])
    d_hidden = mm_t(cot_rows, wo_v[...])

    for t in range(tiles):
        hits_t[t * tile : (t + 1) * tile, :] = hits[:, t * tile : (t + 1) * tile].T
    for t in range(tiles):
        grid_t[:, t * tile : (t + 1) * tile] = grid_v[t * tile : (t + 1) * tile, :].T

    own = pl.ds(pl.multiple_of(me * block, block), block)
    agg_parts = []
    for h in range(2):
        total = part[own, h * half : (h + 1) * half]
        for rel in rels:
            part_copy(h, rel).wait_recv()
            total = total + part_recv[h, rel - 1].astype(F32)
        agg_parts.append(total.astype(BF16))
    agg = jnp.concatenate(agg_parts, axis=1)
    pre_hidden = pre_self + mm(agg, wa_v[...])
    gate = logistic_of(pre_hidden)
    hidden = (pre_hidden * gate).astype(BF16)
    dph = (d_hidden * (gate * (1.0 + pre_hidden * (1.0 - gate)))).astype(BF16)

    def dagg_copy(h, rel):
        return pltpu.make_async_remote_copy(
            src_ref=dagg_all.at[h, own],
            dst_ref=dagg_all.at[h, own],
            send_sem=dagg_ss.at[h, rel - 1],
            recv_sem=dagg_rs.at[h, rel - 1],
            device_id={"band": (me + rel) % bands},
            device_id_type=MESH,
        )

    for h in range(2):
        dagg_all[h, own, :] = mm_t(dph, wa_v[h * half : (h + 1) * half, :]).astype(BF16)
        for rel in rels:
            dagg_copy(h, rel).start()

    def a_copy(b, h):
        return pltpu.make_async_remote_copy(
            src_ref=send_a.at[b, h],
            dst_ref=recv_a.at[b, h],
            send_sem=a_ss.at[b, h],
            recv_sem=a_rs.at[b, h],
            device_id={"dp": core_mate},
            device_id_type=MESH,
        )

    def b_copy(b, h):
        return pltpu.make_async_remote_copy(
            src_ref=send_b.at[b, h],
            dst_ref=recv_b.at[b, h],
            send_sem=b_ss.at[b, h],
            recv_sem=b_rs.at[b, h],
            device_id={"dp": x_mate},
            device_id_type=MESH,
        )

    def c_copy(rel, h):
        other = (me + rel) % bands
        return pltpu.make_async_remote_copy(
            src_ref=send_c.at[other, h],
            dst_ref=recv_c.at[rel - 1, h],
            send_sem=c_ss.at[rel - 1, h],
            recv_sem=c_rs.at[rel - 1, h],
            device_id={"band": other},
            device_id_type=MESH,
        )

    share = width // 4

    def share_of(b, h, x, c):
        return sums[b, h, pl.ds(pl.multiple_of((x * 2 + c) * share, share), share), :]

    def step_a(b, h):
        for x in range(2):
            send_a[b, h, x] = share_of(b, h, x, 1 - core).astype(BF16)
        a_copy(b, h).start()

    def step_b(b, h):
        a_copy(b, h).wait_recv()
        away = 1 - column
        send_b[b, h] = (share_of(b, h, away, core) + recv_a[b, h, away].astype(F32)).astype(BF16)
        b_copy(b, h).start()

    def step_c(b, h):
        kept = share_of(b, h, column, core) + recv_a[b, h, column].astype(F32)
        b_copy(b, h).wait_recv()
        kept = kept + recv_b[b, h].astype(F32)
        total_c[b, h] = kept
        send_c[b, h] = kept.astype(BF16)

    def send_last(h, is_last):
        for rel in rels:
            other = (me + rel) % bands

            @pl.when((other == 3) if is_last else (other != 3))
            def _():
                c_copy(rel, h).start()

    halves = [slice(h * half, (h + 1) * half) for h in range(2)]
    for b, (left, right) in enumerate(((mesh_rows_v, dph), (agg, dph), (hidden, cot_rows))):
        for h in range(2):
            sums[b, h] = row_product(left, right[:, halves[h]])
            step_a(b, h)
    mesh_out_v[...] = (mesh_rows_v.astype(F32) + mm(hidden, wo_v[...])).astype(BF16)
    grad_mesh_v[...] = (cot_rows.astype(F32) + mm_t(dph, ws_v[...])).astype(BF16)
    stores = [
        pltpu.make_async_copy(mesh_out_v, mesh_out_h, out_sem.at[0]),
        pltpu.make_async_copy(grad_mesh_v, grad_mesh_h, out_sem.at[1]),
    ]
    for store in stores:
        store.start()
    for b in range(3):
        for h in range(2):
            step_b(b, h)

    for h in range(2):
        for rel in rels:
            dagg_copy(h, rel).wait_recv()

        @pl.loop(0, tiles // 2)
        def _(t):
            rows = pl.ds(pl.multiple_of(t * (2 * tile), 2 * tile), 2 * tile)
            d_msg = mm(hits_t[rows, :], dagg_all[h])
            dpm[rows, halves[h]] = (d_msg * slope[h, rows, :]).astype(BF16)

        sums[3, h] = mm(grid_t[...], dpm[:, halves[h]])
        step_a(3, h)
        if h == 0:
            step_b(3, 0)
            for g in range(2):
                for b in range(3):
                    step_c(b, g)
                send_last(g, False)

    def gg_store(t):
        rows = pl.ds(pl.multiple_of(t * tile, tile), tile)
        return pltpu.make_async_copy(gg_v.at[rows], grad_grid_h.at[rows], gg_sem.at[t])

    def grid_grads(low, high):
        @pl.loop(low, high)
        def _(t):
            rows = pl.ds(pl.multiple_of(t * tile, tile), tile)
            gg_v[rows, :] = mm_t(dpm[rows, :], wm_v[...]).astype(BF16)
            gg_store(t).start()

    step_c(3, 0)
    send_last(0, True)
    step_b(3, 1)
    grid_grads(0, tiles // 2)
    step_c(3, 1)
    send_last(1, True)
    grid_grads(tiles // 2, tiles)

    for h in range(2):
        total = total_c[me, h]
        for rel in rels:
            c_copy(rel, h).wait_recv()
            total = total + recv_c[rel - 1, h].astype(F32)
        wg_v[:, halves[h]] = total
    stores.append(pltpu.make_async_copy(wg_v, wg_h, out_sem.at[2]))
    stores[2].start()

    @pl.loop(0, tiles)
    def _(t):
        gg_store(t).wait()

    for rel in rels:
        for h in range(2):
            part_copy(h, rel).wait_send()
            dagg_copy(h, rel).wait_send()
            c_copy(rel, h).wait_send()
    for b in range(4):
        for h in range(2):
            a_copy(b, h).wait_send()
            b_copy(b, h).wait_send()
    for store in stores:
        store.wait()


def store_all(chunk, *refs):
    sources, targets, stages, sems = refs[:4], refs[4:8], refs[8:12], refs[12]
    pairs = []
    for source, target, stage in zip(sources, targets, stages):
        for low in range(0, source.shape[0], chunk):
            rows = pl.ds(low, min(chunk, source.shape[0]))
            sem = sems.at[len(pairs)]
            pairs.append(
                (
                    pltpu.make_async_copy(source.at[rows], stage.at[rows], sem),
                    pltpu.make_async_copy(stage.at[rows], target.at[rows], sem),
                )
            )
    for load, _ in pairs:
        load.start()
    for load, store in pairs:
        load.wait()
        store.start()
    for _, store in pairs:
        store.wait()


def fused_shards(
    grid_latent,
    mesh_latent,
    cotangent,
    w_msg,
    w_self,
    w_agg,
    w_out,
    target,
    owner_map,
    pattern,
    live_blocks,
):
    bands = lax.axis_size("band")
    nodes, width = grid_latent.shape[1:]
    block = mesh_latent.shape[1]
    rows = bands * block
    tile = 2 * block
    tiles = nodes // tile
    half = width // 2
    share = width // 4
    anywhere = pl.BlockSpec(memory_space=pl.ANY)
    hbm = pl.BlockSpec(memory_space=pltpu.HBM)
    dma = pltpu.SemaphoreType.DMA
    vmem = pltpu.VMEM
    shapes = (
        jax.ShapeDtypeStruct((block, width), BF16),
        jax.ShapeDtypeStruct((block, width), BF16),
        jax.ShapeDtypeStruct((nodes, width), BF16),
        jax.ShapeDtypeStruct((share, width), F32),
    )
    results = pl.pallas_call(
        functools.partial(fused, bands, tile),
        out_shape=shapes,
        in_specs=[hbm] * 11,
        out_specs=(anywhere,) * 4,
        scratch_shapes=[
            vmem((block, width), BF16),
            vmem((block, width), BF16),
            vmem((nodes, width), BF16),
            vmem((share, width), F32),
            pltpu.SMEM(target.shape[:1], jnp.int32),
            pltpu.SMEM(owner_map.shape, jnp.int32),
            pltpu.SMEM(live_blocks.shape, jnp.int32),
            vmem((2, nodes), jnp.int32),
            vmem((nodes, width), BF16),
            vmem((block, width), BF16),
            vmem((block, width), BF16),
            vmem((width, width), BF16),
            vmem((width, width), BF16),
            vmem((width, width), BF16),
            vmem((width, width), BF16),
            vmem((rows, nodes), BF16),
            vmem((nodes, rows), BF16),
            vmem((width, nodes), BF16),
            vmem((2, nodes, half), BF16),
            vmem((2, nodes, half), F32),
            vmem((rows, width), F32),
            vmem((2, rows, half), BF16),
            vmem((2, bands - 1, block, half), BF16),
            vmem((2, rows, half), BF16),
            vmem((nodes, width), BF16),
            vmem((4, 2, width, half), F32),
            vmem((4, 2, 2, share, half), BF16),
            vmem((4, 2, 2, share, half), BF16),
            vmem((4, 2, share, half), BF16),
            vmem((4, 2, share, half), BF16),
            vmem((4, 2, share, half), BF16),
            vmem((bands - 1, 2, share, half), BF16),
            vmem((4, 2, share, half), F32),
            dma((10,)),
            dma((tiles,)),
            dma((3,)),
            dma((tiles,)),
            dma((2, bands - 1)),
            dma((2, bands - 1)),
            dma((2, bands - 1)),
            dma((2, bands - 1)),
            dma((4, 2)),
            dma((4, 2)),
            dma((4, 2)),
            dma((4, 2)),
            dma((bands - 1, 2)),
            dma((bands - 1, 2)),
        ],
        compiler_params=pltpu.CompilerParams(
            collective_id=0, has_side_effects=True, vmem_limit_bytes=64 * 2**20
        ),
        name="encoder_step",
    )(
        target[:, 0],
        owner_map,
        live_blocks,
        pattern.T,
        grid_latent[0],
        mesh_latent[0],
        cotangent[0],
        w_msg,
        w_self,
        w_agg,
        w_out,
    )
    chunk = 2 * tile
    mesh_out, grad_mesh, grad_grid, weight_grads = pl.pallas_call(
        functools.partial(store_all, chunk),
        out_shape=shapes,
        in_specs=[anywhere] * 4,
        out_specs=(hbm,) * 4,
        scratch_shapes=[vmem(shape.shape, shape.dtype) for shape in shapes]
        + [dma((3 + nodes // chunk,))],
        compiler_params=pltpu.CompilerParams(vmem_limit_bytes=64 * 2**20),
        name="store_results",
    )(*results)
    return mesh_out[None], grad_mesh[None], grad_grid[None], weight_grads


def solution(mesh):
    in_specs = (
        P(("groups", "dp"), "band", None),
        P(("groups", "dp"), "band", None),
        P(("groups", "dp"), "band", None),
        P(),
        P(),
        P(),
        P(),
        P(("groups", "band"), None),
        P("groups"),
        P(("groups", "band"), None),
        P(("groups", "band")),
    )
    out_specs = (
        P(("groups", "dp"), "band", None),
        P(("groups", "dp"), "band", None),
        P(("groups", "dp"), "band", None),
        P(("groups", "band", "dp"), None),
    )
    body = fused_shards if mesh.shape["band"] == 4 and mesh.shape["dp"] == 4 else shards
    return jax.shard_map(body, mesh=mesh, in_specs=in_specs, out_specs=out_specs, check_vma=False)
```
